32 devices in a mesh: groups: 2 (over y), expert: 4 (over z), narrow: 4 (over x, core).
Axes of the slice: x: 2, y: 2, z: 4, core: 2. Of those that a mesh axis runs over, the one named last changes fastest.
Arguments:
- tokens: bfloat16 [256, 3584], P(('groups', 'expert', 'narrow')), parts along dimension 0, may hold values from -6 to 6
- expert_ids: int32 [256, 8], P(('groups', 'expert', 'narrow')), parts along dimension 0, may hold values from 0 to 31, all different within a row; in each aligned block of 32 rows (0 to 31, 32 to 63, ...) at most 13 rows name the same one
- route_weights: bfloat16 [256, 8], P(('groups', 'expert', 'narrow')), parts along dimension 0, may hold values from 0.019897461 to 0.5
- expert_gate: bfloat16 [32, 3584, 2048], P('expert', None, 'narrow'), may hold values from -0.09375 to 0.09375
- expert_up: bfloat16 [32, 3584, 2048], P('expert', None, 'narrow'), may hold values from -0.09375 to 0.09375
- expert_down: bfloat16 [32, 2048, 3584], P('expert', 'narrow'), may hold values from -0.125 to 0.125
- shared_gate: bfloat16 [3584, 10240], P('expert', 'narrow'), may hold values from -0.09375 to 0.09375
- shared_up: bfloat16 [3584, 10240], P('expert', 'narrow'), may hold values from -0.09375 to 0.09375
- shared_down: bfloat16 [10240, 3584], P('narrow', 'expert'), may hold values from -0.0625 to 0.0625
- shared_scale: float32 [3584], replicated, may hold values from -0.09375 to 0.09375
Outputs:
- moe_out: bfloat16 [256, 3584], P(('groups', 'expert', 'narrow')), parts along dimension 0
The draws below stay inside these ranges and needn't reach their ends.
There are 2 independent parts, one for each index of `groups`. The reference program is written for one: setup_inputs(seed, part) draws one part's arguments, and reference() takes and returns one part's arrays. A program takes and returns all parts, laid end to end along the dimension named above; an argument that names none is the same for every part. Nothing has to cross between parts.
Inputs may be any that keep to these rules, and one draw needn't show every extreme that they name: `expert_ids`: each row names 8 different experts. In each aligned block of 32 rows no expert is named by more than 13 rows, and in some block one expert is named by exactly 13 rows.
All inputs are finite; a program needn't handle non-finite values.
Results may differ from the reference program's by a relative error of at most 0.0054.
Values may be sent and summed in bfloat16 or wider, within the bound.
No kernel may reach another device: no remote copies, remote signals or barrier semaphores. Data moves between devices by JAX's collectives and lax.ppermute only.
A program may use at most 256 MiB of HBM per device.

```python
import math
import jax
import jax.numpy as jnp
import numpy as np
from jax import lax

D = 3584
MOE_FF = 2048
SFF = 10240
EXPERTS = 32
TOP = 8
GROUP_ROWS = 32
TOKENS = 128
CAP = 13
N_NARROW = 4


def block_scale(own_key, dims, split, least, top_value):
    gain, own = 1.0, jax.random.fold_in(own_key, 6)
    for dim, parts in split:
        heights = jnp.exp(jax.random.uniform(jax.random.fold_in(own, dim), (parts,), jnp.float32, least / len(split), top_value / len(split)))
        gain = gain * jnp.repeat(heights, dims[dim] // parts).reshape([-1 if axis == dim else 1 for axis in range(len(dims))])
    return gain


def assign_block(rng, own, number, rows, number_of, top, reach, lean):
    order = jax.random.permutation(rng, number_of)
    crowded, common = load_shares(number_of, rows * top, reach, lean, True), load_shares(number_of, rows * top, reach, lean, False)
    places = jnp.arange(number_of)

    def named(tallies, offset_by):
        used = int((tallies > 0).sum())
        fixed = max(1, used // 4)
        shifted = fixed + (places - fixed + offset_by * (used - fixed)) % max(1, number_of - fixed)
        return jnp.zeros((number_of,), jnp.int32).at[order[jnp.where(places < fixed, places, shifted)]].set(jnp.asarray(tallies, jnp.int32))

    tallies = jnp.where(number % 4 == 0, named(crowded, number // 4), named(common, number - number // 4 - 1))
    mixed = jax.random.permutation(jax.random.fold_in(own, 3), number_of)
    giver, sink = mixed[0:number_of // 2 * 2:2], mixed[1:number_of // 2 * 2:2]
    margin = jnp.minimum(tallies[giver] - 1, reach - tallies[sink]) // 2
    margin = jnp.where((giver == order[0]) | (sink == order[0]) | (tallies[sink] == 0), 0, jnp.maximum(margin, 0))
    shifted = jax.random.randint(jax.random.fold_in(own, 4), (number_of // 2,), 0, 1 << 20) % (margin + 1)
    tallies = tallies.at[giver].add(-shifted).at[sink].add(shifted)
    labels = jnp.searchsorted(jnp.cumsum(tallies), jnp.arange(rows * top), side="right").astype(jnp.int32)
    table = labels.reshape(top, rows).T
    table = table[jax.random.permutation(jax.random.fold_in(own, 1), rows)]
    offset_by = jax.random.randint(jax.random.fold_in(own, 2), (rows, 1), 0, top)
    return jnp.take_along_axis(table, (jnp.arange(top)[None, :] + offset_by) % top, axis=1)


def load_shares(amount, total, limit, slope, full):
    loads = [(1 << 20) // math.isqrt(grade ** slope) + 1 for grade in range(1, amount + 1)]
    largest = limit if full else min(limit, max(-(-total // amount), total * loads[0] // sum(loads)))
    least = 1 if total - largest >= amount - 1 else 0
    holding, surplus = [largest] + [least] * (amount - 1), total - largest - least * (amount - 1)
    while surplus > 0:
        movable = [i for i in range(1, amount) if holding[i] < largest] or [i for i in range(1, amount) if holding[i] < limit]
        whole, left = sum([loads[i] for i in movable]), surplus
        for i in movable:
            extra = min(limit - holding[i], max(1, left * loads[i] // whole), surplus)
            holding[i] = holding[i] + extra
            surplus = surplus - extra
    return np.array(holding)


def bell_draw(own_key, shape, deviation, most, cuts=(), kind=jnp.bfloat16):
    values = jax.random.normal(own_key, shape, jnp.float32) * deviation
    if len(cuts) > 0:
        values = block_scale(own_key, shape, cuts, -0.22, 0.18) * values
    return jnp.clip(values, min=-most, max=most).astype(kind)


def setup_inputs(seed: int = 0, part: int = 0) -> dict:
    key_of = jax.random.split(jax.random.key(seed), 11)
    own_keys = jax.random.split(jax.random.fold_in(key_of[10], part), 11)
    tokens = bell_draw(own_keys[0], (TOKENS, D), 1.0, 6.0, ((0, 16),))
    expert_ids_keys = jax.random.split(jax.random.fold_in(own_keys[1], 1), TOKENS // GROUP_ROWS)
    expert_ids_turns = jax.random.permutation(jax.random.fold_in(own_keys[1], 3), TOKENS // GROUP_ROWS)
    expert_ids = jax.vmap(lambda own, number: assign_block(jax.random.fold_in(own_keys[1], 2), own, number, GROUP_ROWS, EXPERTS, TOP, CAP, 2))(expert_ids_keys, expert_ids_turns).reshape((TOKENS, TOP))
    route_weights = jnp.clip(jnp.exp(math.log(0.5) - 3.224016 * jax.random.uniform(own_keys[2], (TOKENS, TOP), jnp.float32) ** block_scale(own_keys[2], (TOKENS, TOP), ((0, 16),), -0.2, 0.2)), 0.019897461, 0.5).astype(jnp.bfloat16)
    expert_gate = bell_draw(key_of[3], (EXPERTS, D, MOE_FF), D ** -0.5, 0.09375, ((0, 4), (2, 4)))
    expert_up = bell_draw(key_of[4], (EXPERTS, D, MOE_FF), D ** -0.5, 0.09375, ((0, 4), (2, 4)))
    expert_down = bell_draw(key_of[5], (EXPERTS, MOE_FF, D), MOE_FF ** -0.5, 0.125, ((0, 4), (1, 4)))
    shared_gate = bell_draw(key_of[6], (D, SFF), D ** -0.5, 0.09375, ((0, 4), (1, 4)))
    shared_up = bell_draw(key_of[7], (D, SFF), D ** -0.5, 0.09375, ((0, 4), (1, 4)))
    shared_down = bell_draw(key_of[8], (SFF, D), SFF ** -0.5, 0.0625, ((0, 4), (1, 4)))
    shared_scale = bell_draw(key_of[9], (D,), D ** -0.5, 0.09375, (), jnp.float32)
    return {"tokens": tokens, "expert_ids": expert_ids, "route_weights": route_weights, "expert_gate": expert_gate, "expert_up": expert_up, "expert_down": expert_down, "shared_gate": shared_gate, "shared_up": shared_up, "shared_down": shared_down, "shared_scale": shared_scale}


def slot_targets(block_ids):
    flat_ids = block_ids.reshape(-1).astype(jnp.int32)
    onehot = (flat_ids[:, None] == jnp.arange(EXPERTS, dtype=jnp.int32)[None, :]).astype(jnp.int32)
    before = jnp.cumsum(onehot, axis=0) - onehot
    return flat_ids * CAP + jnp.sum(before * onehot, axis=1)


def dispatch_block(grouped, block_ids):
    targets = slot_targets(block_ids)
    sources = jnp.arange(targets.shape[0], dtype=jnp.int32) // TOP
    slot_table = jnp.full((EXPERTS * CAP,), grouped.shape[0], jnp.int32).at[targets].set(sources)
    padded = jnp.concatenate([grouped, jnp.zeros((1, grouped.shape[1]), grouped.dtype)], axis=0)
    return padded[slot_table].reshape(EXPERTS, CAP, grouped.shape[1])


def run_expert(operands):
    inputs, w_gate, w_up, w_down = operands
    gate_part = jnp.dot(inputs, w_gate, preferred_element_type=jnp.float32)
    up_part = jnp.dot(inputs, w_up, preferred_element_type=jnp.float32)
    activated = (jax.nn.silu(gate_part) * up_part).astype(jnp.bfloat16)
    pieces = activated.reshape(-1, N_NARROW, MOE_FF // N_NARROW).astype(jnp.float32)
    down_split = w_down.reshape(N_NARROW, MOE_FF // N_NARROW, D).astype(jnp.float32)
    return jnp.einsum('rjf,jfd->jrd', pieces, down_split).astype(jnp.bfloat16)


def combine_block(operands):
    partial_value, block_ids, block_weights = operands
    targets = slot_targets(block_ids)
    picked = partial_value[:, targets].astype(jnp.float32)
    scaled = picked * block_weights.astype(jnp.float32)[None, :, None]
    return jnp.sum(scaled.reshape(N_NARROW, GROUP_ROWS, TOP, D), axis=(0, 2))


def reference(tokens, expert_ids, route_weights, expert_gate, expert_up, expert_down, shared_gate, shared_up, shared_down, shared_scale):
    block_count = TOKENS // GROUP_ROWS
    grouped = tokens.reshape(block_count, GROUP_ROWS, D)
    block_ids = expert_ids.reshape(block_count, GROUP_ROWS, TOP)
    buffers = jax.vmap(dispatch_block)(grouped, block_ids)
    buffers = jnp.swapaxes(buffers, 0, 1).reshape(EXPERTS, block_count * CAP, D)
    outputs = lax.map(run_expert, (buffers, expert_gate, expert_up, expert_down))
    outputs = outputs.reshape(EXPERTS, N_NARROW, block_count, CAP, D)
    outputs = jnp.transpose(outputs, (2, 1, 0, 3, 4)).reshape(block_count, N_NARROW, EXPERTS * CAP, D)
    weights = route_weights.reshape(block_count, GROUP_ROWS * TOP)
    routed = lax.map(combine_block, (outputs, block_ids, weights)).reshape(TOKENS, D)
    gate_total = jnp.dot(tokens, shared_gate, preferred_element_type=jnp.float32)
    up_total = jnp.dot(tokens, shared_up, preferred_element_type=jnp.float32)
    shared_act = (jax.nn.silu(gate_total) * up_total).astype(jnp.bfloat16)
    shared_out = jnp.dot(shared_act, shared_down, preferred_element_type=jnp.float32)
    branch_gate = jax.nn.sigmoid(jnp.dot(tokens.astype(jnp.float32), shared_scale, precision=lax.Precision.HIGHEST))
    return (routed + branch_gate[:, None] * shared_out).astype(jnp.bfloat16)
```

```python
import functools

import jax
import jax.numpy as jnp
from jax import lax
from jax.experimental import pallas as pl
from jax.experimental.pallas import tpu as pltpu
from jax.sharding import PartitionSpec as P

EXPERTS = 32
LANES = 128
VMEM_LIMIT = 48 * 2**20


def chunk_of(width, most):
    best = width
    for size in range(LANES, most + 1, LANES):
        if width % size == 0:
            best = size
    return best


def z_shift(value, step):
    spread = lax.axis_size("expert")
    return lax.ppermute(value, "expert", [(i, (i + step) % spread) for i in range(spread)])


def x_shift(value, step):
    size = lax.axis_size("narrow")
    return lax.ppermute(value, "narrow", [(i, (i + 2 * step) % size) for i in range(size)])


def core_swap(value):
    size = lax.axis_size("narrow")
    return lax.ppermute(value, "narrow", [(i, i ^ 1) for i in range(size)])


def gather_rows(own):
    spread, chips = lax.axis_size("expert"), lax.axis_size("narrow") // 2
    column = jnp.concatenate([own] + [z_shift(own, d) for d in range(1, spread)], axis=0)
    plane = jnp.concatenate([column] + [x_shift(column, d) for d in range(1, chips)], axis=0)
    return jnp.concatenate([plane, core_swap(plane)], axis=0)


def shared_in_kernel(sizes, x_ref, gate_ref, up_ref, *out_refs):
    outer, spread, rows = sizes
    x = x_ref[...]
    for half, w_ref in enumerate((gate_ref, up_ref)):
        sums = jnp.dot(x, w_ref[...], preferred_element_type=jnp.float32)
        sums = sums.reshape(outer, spread, rows, sums.shape[1])
        for d in range(spread):
            block = sums[:, d].reshape(outer * rows, sums.shape[3])
            out_refs[d][half] = block.astype(jnp.bfloat16)


def shared_in(x, gate, up, rows):
    count, depth = x.shape
    hidden = gate.shape[1]
    spread = lax.axis_size("expert")
    outer = count // (spread * rows)
    width = chunk_of(hidden, 512)
    w_spec = pl.BlockSpec((depth, width), lambda j: (0, j))
    out_spec = pl.BlockSpec((2, outer * rows, width), lambda j: (0, 0, j))
    return pl.pallas_call(
        functools.partial(shared_in_kernel, (outer, spread, rows)),
        grid=(hidden // width,),
        in_specs=[pl.BlockSpec((count, depth), lambda j: (0, 0)), w_spec, w_spec],
        out_specs=[out_spec] * spread,
        out_shape=[jax.ShapeDtypeStruct((2, outer * rows, hidden), jnp.bfloat16)] * spread,
        compiler_params=pltpu.CompilerParams(vmem_limit_bytes=VMEM_LIMIT),
        cost_estimate=pl.CostEstimate(
            flops=4 * count * depth * hidden,
            bytes_accessed=4 * depth * hidden + 4 * count * hidden,
            transcendentals=0,
        ),
        name="shared_in",
    )(x, gate, up)


def expert_in_kernel(feat, first_ref, x_ref, gate_ref, up_ref, out_ref):
    chosen = first_ref[0] + pl.program_id(0)
    x = x_ref[:, :feat]
    gate = jnp.dot(x, gate_ref[0], preferred_element_type=jnp.float32)
    up = jnp.dot(x, up_ref[0], preferred_element_type=jnp.float32)
    table = x_ref[:, feat:].astype(jnp.float32)
    lane = lax.broadcasted_iota(jnp.int32, table.shape, 1)
    weight = jnp.sum(jnp.where(lane == chosen, table, 0.0), axis=1, keepdims=True)
    value = gate / (1.0 + jnp.exp(-gate)) * up * weight
    out_ref[...] = jnp.where(weight == 0.0, 0.0, value).astype(jnp.bfloat16)


def expert_in(x, gate, up, first):
    count, wide = x.shape
    local, feat, hidden = gate.shape
    w_spec = pl.BlockSpec((1, feat, hidden), lambda i: (i, 0, 0))
    return pl.pallas_call(
        functools.partial(expert_in_kernel, feat),
        grid=(local,),
        in_specs=[
            pl.BlockSpec(memory_space=pltpu.SMEM),
            pl.BlockSpec((count, wide), lambda i: (0, 0)),
            w_spec,
            w_spec,
        ],
        out_specs=pl.BlockSpec((count, hidden), lambda i: (0, i)),
        out_shape=jax.ShapeDtypeStruct((count, local * hidden), jnp.bfloat16),
        compiler_params=pltpu.CompilerParams(vmem_limit_bytes=VMEM_LIMIT),
        cost_estimate=pl.CostEstimate(
            flops=4 * count * local * feat * hidden,
            bytes_accessed=4 * local * feat * hidden,
            transcendentals=count * local * hidden,
        ),
        name="expert_in",
    )(first, x, gate, up)


def expert_out_kernel(act_ref, down_ref, keep_ref, send_ref):
    local, hidden, width = down_ref.shape
    sums = jnp.dot(
        act_ref[...],
        down_ref[...].reshape(local * hidden, width),
        preferred_element_type=jnp.float32,
    )
    half = sums.shape[0] // 2
    keep_ref[...] = sums[:half]
    send_ref[...] = sums[half:].astype(jnp.bfloat16)


def expert_out(act, down):
    count = act.shape[0]
    local, hidden, feat = down.shape
    width = chunk_of(feat, 512)
    out_spec = pl.BlockSpec((count // 2, width), lambda j: (0, j))
    return pl.pallas_call(
        expert_out_kernel,
        grid=(feat // width,),
        in_specs=[
            pl.BlockSpec(act.shape, lambda j: (0, 0)),
            pl.BlockSpec((local, hidden, width), lambda j: (0, 0, j)),
        ],
        out_specs=[out_spec, out_spec],
        out_shape=[
            jax.ShapeDtypeStruct((count // 2, feat), jnp.float32),
            jax.ShapeDtypeStruct((count // 2, feat), jnp.bfloat16),
        ],
        compiler_params=pltpu.CompilerParams(vmem_limit_bytes=VMEM_LIMIT),
        cost_estimate=pl.CostEstimate(
            flops=2 * count * local * hidden * feat,
            bytes_accessed=2 * local * hidden * feat,
            transcendentals=0,
        ),
        name="expert_out",
    )(act, down)


def shared_out_kernel(sizes, feat, x_ref, scale_ref, down_ref, *refs):
    outer, spread, rows = sizes
    act_refs, (keep_ref, send_ref) = refs[:spread], refs[spread:]
    parts = [
        jnp.dot(act[...], down_ref[...], preferred_element_type=jnp.float32) for act in act_refs
    ]
    sums = jnp.stack([part.reshape(outer, rows, part.shape[1]) for part in parts], axis=1)
    sums = sums.reshape(outer * spread * rows, sums.shape[3])
    inner = jnp.sum(
        x_ref[:, :feat].astype(jnp.float32) * scale_ref[...], axis=1, keepdims=True
    )
    sums = sums / (1.0 + jnp.exp(-inner))
    half = sums.shape[0] // 2
    keep_ref[...] = sums[:half]
    send_ref[...] = sums[half:]


def shared_out(x, scale, down, acts, rows):
    count, spread = x.shape[0], len(acts)
    outer = count // (spread * rows)
    out = jax.ShapeDtypeStruct((count // 2, down.shape[1]), jnp.float32)
    return pl.pallas_call(
        functools.partial(shared_out_kernel, (outer, spread, rows), scale.shape[0]),
        out_shape=[out, out],
        compiler_params=pltpu.CompilerParams(vmem_limit_bytes=VMEM_LIMIT),
        cost_estimate=pl.CostEstimate(
            flops=2 * count * down.shape[0] * down.shape[1],
            bytes_accessed=2 * down.shape[0] * down.shape[1],
            transcendentals=count,
        ),
        name="shared_out",
    )(x, scale.reshape(1, -1), down, *acts)


def narrow_sum(keep, send, kind):
    chips = lax.axis_size("narrow") // 2
    total = keep + core_swap(send).astype(jnp.float32)
    part = total.shape[0] // chips
    result = total[:part]
    for d in range(1, chips):
        result = result + x_shift(total[d * part : (d + 1) * part].astype(kind), -d).astype(
            jnp.float32
        )
    return result


def body(
    tokens,
    expert_ids,
    route_weights,
    expert_gate,
    expert_up,
    expert_down,
    shared_gate,
    shared_up,
    shared_down,
    shared_scale,
):
    rows, feat = tokens.shape
    spread = lax.axis_size("expert")
    here = lax.axis_index("expert")
    local = expert_gate.shape[0]
    lane = jnp.arange(LANES, dtype=jnp.int32)
    table = jnp.sum(
        jnp.where(
            expert_ids[:, :, None] == lane, route_weights[:, :, None].astype(jnp.float32), 0.0
        ),
        axis=1,
    ).astype(jnp.bfloat16)
    x = gather_rows(jnp.concatenate([tokens, table], axis=1))

    depth = shared_gate.shape[0]
    x_part = lax.dynamic_slice_in_dim(x, here * depth, depth, axis=1)
    hidden_parts = shared_in(x_part, shared_gate, shared_up, rows)
    hidden = hidden_parts[0].astype(jnp.float32)
    for d in range(1, spread):
        hidden = hidden + z_shift(hidden_parts[d], -d).astype(jnp.float32)
    shared_act = (jax.nn.silu(hidden[0]) * hidden[1]).astype(jnp.bfloat16)
    acts = [shared_act] + [z_shift(shared_act, d) for d in range(1, spread)]

    first = (here * local).astype(jnp.int32).reshape(1)
    act = expert_in(x, expert_gate, expert_up, first)
    routed = narrow_sum(*expert_out(act, expert_down), jnp.bfloat16)
    total = routed[:rows]
    for d in range(1, spread):
        total = total + z_shift(
            routed[d * rows : (d + 1) * rows].astype(jnp.bfloat16), -d
        ).astype(jnp.float32)

    part = narrow_sum(*shared_out(x, shared_scale, shared_down, acts, rows), jnp.float32)
    width = part.shape[1]
    for d in range(spread):
        piece = part[:rows] if d == 0 else z_shift(part[d * rows : (d + 1) * rows], -d)
        at = lax.rem(here + d, spread) * width
        old = lax.dynamic_slice_in_dim(total, at, width, axis=1)
        total = lax.dynamic_update_slice_in_dim(total, old + piece, at, axis=1)
    return total.astype(jnp.bfloat16)


def solution(mesh):
    return jax.shard_map(
        body,
        mesh=mesh,
        in_specs=(
            P(("groups", "expert", "narrow"), None),
            P(("groups", "expert", "narrow"), None),
            P(("groups", "expert", "narrow"), None),
            P("expert", None, "narrow"),
            P("expert", None, "narrow"),
            P("expert", "narrow", None),
            P("expert", "narrow"),
            P("expert", "narrow"),
            P("narrow", "expert"),
            P(),
        ),
        out_specs=P(("groups", "expert", "narrow"), None),
        check_vma=False,
    )
```

```python
import functools

import jax
import jax.numpy as jnp
from jax import lax
from jax.experimental import pallas as pl
from jax.experimental.pallas import tpu as pltpu
from jax.sharding import PartitionSpec as P

EXPERTS = 32
LANES = 128
VMEM_LIMIT = 48 * 2**20
VMEM_WHOLE = 60 * 2**20


def chunk_of(width, most):
    best = width
    for size in range(LANES, most + 1, LANES):
        if width % size == 0:
            best = size
    return best


def z_shift(value, step):
    spread = lax.axis_size("expert")
    return lax.ppermute(value, "expert", [(i, (i + step) % spread) for i in range(spread)])


def x_shift(value, step):
    size = lax.axis_size("narrow")
    return lax.ppermute(value, "narrow", [(i, (i + 2 * step) % size) for i in range(size)])


def core_swap(value):
    size = lax.axis_size("narrow")
    return lax.ppermute(value, "narrow", [(i, i ^ 1) for i in range(size)])


def gather_column(pieces):
    return [pieces[0]] + [z_shift(piece, d) for d, piece in enumerate(pieces) if d > 0]


def gather_plane(column):
    chips = lax.axis_size("narrow") // 2
    return [column] + [x_shift(column, d) for d in range(1, chips)]


def both_cores(plane):
    return jnp.concatenate([plane, core_swap(plane)], axis=0)


def join(*lists):
    values = iter(lax.optimization_barrier([value for part in lists for value in part]))
    return [[next(values) for _ in part] for part in lists]


def stream(source, buffer, sems, width, first=0):
    copies = []
    for j in range(buffer.shape[-1] // width):
        lead = (slice(None),) * (len(buffer.shape) - 1)
        copies.append(
            pltpu.make_async_copy(
                source.at[lead + (pl.ds(first + j * width, width),)],
                buffer.at[lead + (pl.ds(j * width, width),)],
                sems.at[j],
            )
        )
        copies[-1].start()
    return copies


def prepare_kernel(tokens_ref, ids_ref, weights_ref, out_ref):
    feat = tokens_ref.shape[1]
    ids = ids_ref[...]
    weights = weights_ref[...].astype(jnp.float32)
    lane = lax.broadcasted_iota(jnp.int32, (ids.shape[0], LANES), 1)
    table = jnp.zeros(lane.shape, jnp.float32)
    for k in range(ids.shape[1]):
        table = jnp.where(lane == ids[:, k : k + 1], weights[:, k : k + 1], table)
    out_ref[:, :feat] = tokens_ref[...]
    out_ref[:, feat:] = table.astype(jnp.bfloat16)


def prepare(tokens, ids, weights):
    rows, feat = tokens.shape
    return pl.pallas_call(
        prepare_kernel,
        out_shape=jax.ShapeDtypeStruct((rows, feat + LANES), jnp.bfloat16),
        compiler_params=pltpu.CompilerParams(vmem_limit_bytes=VMEM_WHOLE),
        cost_estimate=pl.CostEstimate(
            flops=0, bytes_accessed=4 * tokens.size, transcendentals=0
        ),
        name="prepare",
    )(tokens, ids, weights)


def shared_in_kernel(sizes, width, gate_ref, up_ref, *refs):
    outer, spread, rows = sizes
    x_refs, out_refs = refs[:outer], refs[outer : outer + spread]
    gate_buf, up_buf, sems = refs[outer + spread :]
    work = []
    for half, (ref, buf) in enumerate(((gate_ref, gate_buf), (up_ref, up_buf))):
        work.append((half, buf, pltpu.make_async_copy(ref, buf, sems.at[half])))
        work[-1][2].start()
    x = jnp.concatenate([ref[...].astype(jnp.float32) for ref in x_refs], axis=0)
    x = x.astype(jnp.bfloat16)
    for half, buf, copy in work:
        copy.wait()
        for j in range(buf.shape[1] // width):
            columns = pl.ds(j * width, width)
            sums = jnp.dot(x, buf[:, columns], preferred_element_type=jnp.float32)
            sums = sums.reshape(outer, spread, rows, width)
            for d in range(spread):
                block = sums[:, d].reshape(outer * rows, width)
                out_refs[d][half, :, columns] = block.astype(jnp.bfloat16)


def shared_in(pieces, gate, up, rows):
    depth, hidden = gate.shape
    outer, spread = len(pieces), lax.axis_size("expert")
    count = outer * spread * rows
    whole = pl.BlockSpec(memory_space=pltpu.VMEM)
    apart = pl.BlockSpec(memory_space=pl.ANY)
    return pl.pallas_call(
        functools.partial(shared_in_kernel, (outer, spread, rows), chunk_of(hidden, 512)),
        in_specs=[apart, apart] + [whole] * outer,
        out_shape=[jax.ShapeDtypeStruct((2, outer * rows, hidden), jnp.bfloat16)] * spread,
        scratch_shapes=[pltpu.VMEM(gate.shape, gate.dtype)] * 2 + [pltpu.SemaphoreType.DMA((2,))],
        compiler_params=pltpu.CompilerParams(vmem_limit_bytes=VMEM_WHOLE),
        cost_estimate=pl.CostEstimate(
            flops=4 * count * depth * hidden,
            bytes_accessed=4 * depth * hidden + 4 * count * hidden,
            transcendentals=0,
        ),
        name="shared_in",
    )(gate, up, *pieces)


def expert_in_kernel(feat, first_ref, x_ref, scale_ref, gate_ref, up_ref, out_ref, branch_ref):
    @pl.when(pl.program_id(0) == 0)
    def _():
        inner = jnp.sum(
            x_ref[:, :feat].astype(jnp.float32) * scale_ref[...], axis=1, keepdims=True
        )
        branch_ref[...] = jnp.broadcast_to(1.0 / (1.0 + jnp.exp(-inner)), branch_ref.shape)

    chosen = first_ref[0] + pl.program_id(0)
    x = x_ref[:, :feat]
    gate = jnp.dot(x, gate_ref[0], preferred_element_type=jnp.float32)
    up = jnp.dot(x, up_ref[0], preferred_element_type=jnp.float32)
    table = x_ref[:, feat:].astype(jnp.float32)
    lane = lax.broadcasted_iota(jnp.int32, table.shape, 1)
    weight = jnp.sum(jnp.where(lane == chosen, table, 0.0), axis=1, keepdims=True)
    value = gate / (1.0 + jnp.exp(-gate)) * up * weight
    out_ref[...] = jnp.where(weight == 0.0, 0.0, value).astype(jnp.bfloat16)


def expert_in(x, scale, gate, up, first):
    count, wide = x.shape
    local, feat, hidden = gate.shape
    w_spec = pl.BlockSpec((1, feat, hidden), lambda i: (i, 0, 0))
    return pl.pallas_call(
        functools.partial(expert_in_kernel, feat),
        grid=(local,),
        in_specs=[
            pl.BlockSpec(memory_space=pltpu.SMEM),
            pl.BlockSpec((count, wide), lambda i: (0, 0)),
            pl.BlockSpec((1, feat), lambda i: (0, 0)),
            w_spec,
            w_spec,
        ],
        out_specs=[
            pl.BlockSpec((count, hidden), lambda i: (0, i)),
            pl.BlockSpec((count, LANES), lambda i: (0, 0)),
        ],
        out_shape=[
            jax.ShapeDtypeStruct((count, local * hidden), jnp.bfloat16),
            jax.ShapeDtypeStruct((count, LANES), jnp.float32),
        ],
        compiler_params=pltpu.CompilerParams(vmem_limit_bytes=VMEM_LIMIT),
        cost_estimate=pl.CostEstimate(
            flops=4 * count * local * feat * hidden,
            bytes_accessed=4 * local * feat * hidden,
            transcendentals=count * local * hidden,
        ),
        name="expert_in",
    )(first, x, scale.reshape(1, feat), gate, up)


def expert_out_kernel(first, width, act_ref, down_ref, keep_ref, send_ref, buf, sems):
    local, hidden, columns = buf.shape
    copies = stream(down_ref, buf, sems, width, first)
    act = act_ref[...]
    half = act.shape[0] // 2
    for j, copy in enumerate(copies):
        at = pl.ds(j * width, width)
        copy.wait()
        sums = jnp.dot(
            act, buf[:, :, at].reshape(local * hidden, width), preferred_element_type=jnp.float32
        )
        keep_ref[:, at] = sums[:half]
        send_ref[:, at] = sums[half:].astype(jnp.bfloat16)


def expert_out(act, down, first, columns):
    count = act.shape[0]
    local, hidden, _ = down.shape
    width = chunk_of(columns, 256)
    whole = pl.BlockSpec(memory_space=pltpu.VMEM)
    return pl.pallas_call(
        functools.partial(expert_out_kernel, first, width),
        in_specs=[whole, pl.BlockSpec(memory_space=pl.ANY)],
        out_specs=[whole, whole],
        out_shape=[
            jax.ShapeDtypeStruct((count // 2, columns), jnp.float32),
            jax.ShapeDtypeStruct((count // 2, columns), jnp.bfloat16),
        ],
        scratch_shapes=[
            pltpu.VMEM((local, hidden, columns), down.dtype),
            pltpu.SemaphoreType.DMA((columns // width,)),
        ],
        compiler_params=pltpu.CompilerParams(vmem_limit_bytes=VMEM_LIMIT),
        cost_estimate=pl.CostEstimate(
            flops=2 * count * local * hidden * columns,
            bytes_accessed=2 * local * hidden * columns,
            transcendentals=0,
        ),
        name="expert_out",
    )(act, down)


def shared_out_kernel(sizes, branch_ref, down_ref, *refs):
    outer, spread, rows = sizes
    act_refs, (keep_ref, send_ref) = refs[:spread], refs[spread:]
    act = jnp.concatenate([ref[...] for ref in act_refs], axis=0)
    sums = jnp.dot(act, down_ref[...], preferred_element_type=jnp.float32)
    width = sums.shape[1]
    sums = jnp.swapaxes(sums.reshape(spread, outer, rows, width), 0, 1)
    sums = sums.reshape(outer * spread * rows, width) * branch_ref[:, :1]
    half = sums.shape[0] // 2
    keep_ref[...] = sums[:half]
    send_ref[...] = sums[half:]


def shared_out(branch, down, acts, rows):
    count, spread = branch.shape[0], len(acts)
    outer = count // (spread * rows)
    out = jax.ShapeDtypeStruct((count // 2, down.shape[1]), jnp.float32)
    return pl.pallas_call(
        functools.partial(shared_out_kernel, (outer, spread, rows)),
        out_shape=[out, out],
        compiler_params=pltpu.CompilerParams(vmem_limit_bytes=VMEM_LIMIT),
        cost_estimate=pl.CostEstimate(
            flops=2 * count * down.shape[0] * down.shape[1],
            bytes_accessed=2 * down.shape[0] * down.shape[1],
            transcendentals=0,
        ),
        name="shared_out",
    )(branch, down, *acts)


def narrow_sum(keep, send, kind):
    chips = lax.axis_size("narrow") // 2
    total = keep + core_swap(send).astype(jnp.float32)
    part = total.shape[0] // chips
    result = total[:part]
    for d in range(1, chips):
        result = result + x_shift(total[d * part : (d + 1) * part].astype(kind), -d).astype(
            jnp.float32
        )
    return result


def body(
    tokens,
    expert_ids,
    route_weights,
    expert_gate,
    expert_up,
    expert_down,
    shared_gate,
    shared_up,
    shared_down,
    shared_scale,
):
    rows, feat = tokens.shape
    spread = lax.axis_size("expert")
    here = lax.axis_index("expert")
    local = expert_gate.shape[0]
    depth = shared_gate.shape[0]
    own = prepare(tokens, expert_ids, route_weights)
    column = jnp.concatenate(gather_column([own] * spread), axis=0)
    part = lax.dynamic_slice_in_dim(column, here * depth, depth, axis=1)
    parts, (column,) = join(gather_plane(part), [column])
    parts = parts + [core_swap(piece) for piece in parts]
    hidden_parts = shared_in(parts, shared_gate, shared_up, rows)
    plane, hidden_parts = join(gather_plane(column), hidden_parts)
    x = both_cores(jnp.concatenate(plane, axis=0))

    first = (here * local).astype(jnp.int32).reshape(1)
    act, branch = expert_in(x, shared_scale, expert_gate, expert_up, first)
    middle = feat // LANES // 2 * LANES
    keep, send = expert_out(act, expert_down, 0, middle)
    arrived = [z_shift(hidden_parts[d], -d) for d in range(1, spread)]
    arrived, (keep, send) = join(arrived, [keep, send])
    hidden = hidden_parts[0].astype(jnp.float32)
    for piece in arrived:
        hidden = hidden + piece.astype(jnp.float32)
    shared_act = (jax.nn.silu(hidden[0]) * hidden[1]).astype(jnp.bfloat16)
    (act,), (shared_act,) = join([act], [shared_act])
    acts = gather_column([shared_act] * spread)
    left = narrow_sum(keep, send, jnp.bfloat16)
    right = expert_out(act, expert_down, middle, feat - middle)
    acts, right, (left,) = join(acts, right, [left])
    right = narrow_sum(*right, jnp.bfloat16)
    routed = jnp.concatenate([left, right], axis=1)

    part = narrow_sum(*shared_out(branch, shared_down, acts, rows), jnp.float32)
    both = jnp.concatenate([routed, part], axis=1)
    pieces = [both[:rows]] + [
        z_shift(both[d * rows : (d + 1) * rows].astype(jnp.bfloat16), -d).astype(jnp.float32)
        for d in range(1, spread)
    ]
    total = pieces[0][:, :feat]
    for piece in pieces[1:]:
        total = total + piece[:, :feat]
    width = part.shape[1]
    for d, piece in enumerate(pieces):
        at = lax.rem(here + d, spread) * width
        old = lax.dynamic_slice_in_dim(total, at, width, axis=1)
        total = lax.dynamic_update_slice_in_dim(total, old + piece[:, feat:], at, axis=1)
    return total.astype(jnp.bfloat16)


def solution(mesh):
    return jax.shard_map(
        body,
        mesh=mesh,
        in_specs=(
            P(("groups", "expert", "narrow"), None),
            P(("groups", "expert", "narrow"), None),
            P(("groups", "expert", "narrow"), None),
            P("expert", None, "narrow"),
            P("expert", None, "narrow"),
            P("expert", "narrow", None),
            P("expert", "narrow"),
            P("expert", "narrow"),
            P("narrow", "expert"),
            P(),
        ),
        out_specs=P(("groups", "expert", "narrow"), None),
        check_vma=False,
    )
```

```python
import functools
import math

import jax
import jax.numpy as jnp
from jax import lax
from jax.experimental import pallas as pl
from jax.experimental.pallas import tpu as pltpu
from jax.sharding import PartitionSpec as P

EXPERTS = 32
LANES = 128
VMEM_LIMIT = 48 * 2**20
VMEM_SMALL = 8 * 2**20


def chunk_of(width, most):
    best = width
    for size in range(LANES, most + 1, LANES):
        if width % size == 0:
            best = size
    return best


def z_shift(value, step):
    spread = lax.axis_size("expert")
    return lax.ppermute(value, "expert", [(i, (i + step) % spread) for i in range(spread)])


def x_shift(value, step):
    size = lax.axis_size("narrow")
    return lax.ppermute(value, "narrow", [(i, (i + 2 * step) % size) for i in range(size)])


def core_swap(value):
    size = lax.axis_size("narrow")
    return lax.ppermute(value, "narrow", [(i, i ^ 1) for i in range(size)])


def gather_column(pieces):
    return [pieces[0]] + [z_shift(piece, d) for d, piece in enumerate(pieces) if d > 0]


def gather_plane(column):
    chips = lax.axis_size("narrow") // 2
    return [column] + [x_shift(column, d) for d in range(1, chips)]


def both_cores(plane):
    return jnp.concatenate([plane, core_swap(plane)], axis=0)


def join(*lists):
    values = iter(lax.optimization_barrier([value for part in lists for value in part]))
    return [[next(values) for _ in part] for part in lists]


def load_kernel(*refs):
    count = len(refs) // 2
    sources, targets, sems = refs[:count], refs[count:-1], refs[-1]
    copies = [
        pltpu.make_async_copy(source.at[pl.ds(0, target.shape[0])], target, sems.at[i])
        for i, (source, target) in enumerate(zip(sources, targets))
    ]
    for copy in copies:
        copy.start()
    for copy in copies:
        copy.wait()


def load(arrays, taken):
    shapes = [(taken, *value.shape[1:]) for value in arrays]
    return pl.pallas_call(
        load_kernel,
        in_specs=[pl.BlockSpec(memory_space=pl.ANY)] * len(arrays),
        out_shape=[
            jax.ShapeDtypeStruct(shape, value.dtype) for shape, value in zip(shapes, arrays)
        ],
        scratch_shapes=[pltpu.SemaphoreType.DMA((len(arrays),))],
        compiler_params=pltpu.CompilerParams(vmem_limit_bytes=VMEM_SMALL),
        cost_estimate=pl.CostEstimate(
            flops=0,
            bytes_accessed=sum(2 * math.prod(shape) for shape in shapes),
            transcendentals=0,
        ),
        name="load",
    )(*arrays)


def shared_in_kernel(sizes, width, gate_ref, up_ref, *refs):
    outer, spread, rows = sizes
    x_refs, out_refs = refs[:outer], refs[outer : outer + spread]
    x_buf, sems = refs[outer + spread :]
    copies = [
        pltpu.make_async_copy(ref, x_buf.at[i], sems.at[i]) for i, ref in enumerate(x_refs)
    ]
    for copy in copies:
        copy.start()
    for copy in copies:
        copy.wait()
    x = x_buf[...].reshape(outer * spread * rows, x_buf.shape[2])
    for half, ref in enumerate((gate_ref, up_ref)):
        for j in range(ref.shape[1] // width):
            columns = pl.ds(j * width, width)
            sums = jnp.dot(x, ref[:, columns], preferred_element_type=jnp.float32)
            sums = sums.reshape(outer, spread, rows, width)
            for d in range(spread):
                block = sums[:, d].reshape(outer * rows, width)
                out_refs[d][half, :, columns] = block.astype(jnp.bfloat16)


def shared_in(pieces, gate, up, rows):
    depth, hidden = gate.shape
    outer, spread = len(pieces), lax.axis_size("expert")
    count = outer * spread * rows
    whole = pl.BlockSpec(memory_space=pltpu.VMEM)
    apart = pl.BlockSpec(memory_space=pl.ANY)
    return pl.pallas_call(
        functools.partial(shared_in_kernel, (outer, spread, rows), chunk_of(hidden, 512)),
        in_specs=[whole, whole] + [apart] * outer,
        out_shape=[jax.ShapeDtypeStruct((2, outer * rows, hidden), jnp.bfloat16)] * spread,
        scratch_shapes=[
            pltpu.VMEM((outer, spread * rows, depth), gate.dtype),
            pltpu.SemaphoreType.DMA((outer,)),
        ],
        compiler_params=pltpu.CompilerParams(vmem_limit_bytes=VMEM_SMALL),
        cost_estimate=pl.CostEstimate(
            flops=4 * count * depth * hidden,
            bytes_accessed=4 * count * hidden,
            transcendentals=0,
        ),
        name="shared_in",
    )(gate, up, *pieces)


def experts_kernel(chosen, first_ref, x_ref, scale_ref, gate_ref, up_ref, down_ref, *refs):
    branch_ref, keep_ref, send_ref = refs[:3]
    act_buf, gate_buf, up_buf, down_buf, sems, down_sems = refs[3:]
    local, feat, hidden = gate_ref.shape
    slots, (down_slots, _, _, width) = gate_buf.shape[0], down_buf.shape
    blocks = feat // width

    def copies(i):
        slot = i % slots
        return [
            pltpu.make_async_copy(ref.at[i], buf.at[slot], sems.at[half, slot])
            for half, (ref, buf) in enumerate(((gate_ref, gate_buf), (up_ref, up_buf)))
        ]

    def down_copy(j):
        slot = j % down_slots
        return pltpu.make_async_copy(
            down_ref.at[:, :, pl.ds(j * width, width)], down_buf.at[slot], down_sems.at[slot]
        )

    for i in range(slots):
        for copy in copies(i):
            copy.start()
    inner = jnp.sum(x_ref[:, :feat].astype(jnp.float32) * scale_ref[...], axis=1, keepdims=True)
    branch_ref[...] = jnp.broadcast_to(1.0 / (1.0 + jnp.exp(-inner)), branch_ref.shape)
    route = x_ref[:, feat:].astype(jnp.float32)
    named, weights = route[:, :chosen], route[:, chosen : 2 * chosen]
    x = x_ref[:, :feat]
    for i in range(local):
        slot = i % slots
        gate_copy, up_copy = copies(i)
        gate_copy.wait()
        gate = jnp.dot(x, gate_buf[slot], preferred_element_type=jnp.float32)
        up_copy.wait()
        up = jnp.dot(x, up_buf[slot], preferred_element_type=jnp.float32)
        if i + slots < local:
            for copy in copies(i + slots):
                copy.start()
        if i == max(local - slots, 0):
            for j in range(down_slots):
                down_copy(j).start()
        expert = (first_ref[0] + i).astype(jnp.float32)
        weight = jnp.sum(jnp.where(named == expert, weights, 0.0), axis=1, keepdims=True)
        value = gate / (1.0 + jnp.exp(-gate)) * up * weight
        act_buf[:, i * hidden : (i + 1) * hidden] = jnp.where(
            weight == 0.0, 0.0, value
        ).astype(jnp.bfloat16)
    half = act_buf.shape[0] // 2
    for j in range(blocks):
        down_copy(j).wait()
        sums = jnp.dot(
            act_buf[...],
            down_buf[j % down_slots].reshape(local * hidden, width),
            preferred_element_type=jnp.float32,
        )
        if j + down_slots < blocks:
            down_copy(j + down_slots).start()
        at = pl.ds(j * width, width)
        keep_ref[:, at] = sums[:half]
        send_ref[:, at] = sums[half:].astype(jnp.bfloat16)


def experts(x, scale, gate, up, down, first, chosen):
    count = x.shape[0]
    local, feat, hidden = gate.shape
    whole = pl.BlockSpec(memory_space=pltpu.VMEM)
    apart = pl.BlockSpec(memory_space=pl.ANY)
    slots = min(3, local)
    width = chunk_of(feat, 256)
    down_slots = (feat // width + 1) // 2
    buffer = pltpu.VMEM((slots, feat, hidden), gate.dtype)
    return pl.pallas_call(
        functools.partial(experts_kernel, chosen),
        in_specs=[pl.BlockSpec(memory_space=pltpu.SMEM), whole, whole, apart, apart, apart],
        out_shape=[
            jax.ShapeDtypeStruct((count, LANES), jnp.float32),
            jax.ShapeDtypeStruct((count // 2, feat), jnp.float32),
            jax.ShapeDtypeStruct((count // 2, feat), jnp.bfloat16),
        ],
        scratch_shapes=[
            pltpu.VMEM((count, local * hidden), jnp.bfloat16),
            buffer,
            buffer,
            pltpu.VMEM((down_slots, local, hidden, width), down.dtype),
            pltpu.SemaphoreType.DMA((2, slots)),
            pltpu.SemaphoreType.DMA((down_slots,)),
        ],
        compiler_params=pltpu.CompilerParams(vmem_limit_bytes=VMEM_LIMIT),
        cost_estimate=pl.CostEstimate(
            flops=6 * count * local * feat * hidden,
            bytes_accessed=6 * local * feat * hidden,
            transcendentals=count * local * hidden,
        ),
        name="experts",
    )(first, x, scale.reshape(1, feat), gate, up, down)


def shared_out_kernel(sizes, branch_ref, down_ref, *refs):
    outer, spread, rows = sizes
    act_refs, (keep_ref, send_ref) = refs[:spread], refs[spread:]
    act = jnp.concatenate([ref[...] for ref in act_refs], axis=0)
    sums = jnp.dot(act, down_ref[...], preferred_element_type=jnp.float32)
    width = sums.shape[1]
    sums = jnp.swapaxes(sums.reshape(spread, outer, rows, width), 0, 1)
    sums = sums.reshape(outer * spread * rows, width) * branch_ref[:, :1]
    half = sums.shape[0] // 2
    keep_ref[...] = sums[:half]
    send_ref[...] = sums[half:].astype(jnp.bfloat16)


def shared_out(branch, down, acts, rows):
    count, spread = branch.shape[0], len(acts)
    outer = count // (spread * rows)
    shape = (count // 2, down.shape[1])
    return pl.pallas_call(
        functools.partial(shared_out_kernel, (outer, spread, rows)),
        out_shape=[
            jax.ShapeDtypeStruct(shape, jnp.float32),
            jax.ShapeDtypeStruct(shape, jnp.bfloat16),
        ],
        compiler_params=pltpu.CompilerParams(vmem_limit_bytes=VMEM_LIMIT),
        cost_estimate=pl.CostEstimate(
            flops=2 * count * down.shape[0] * down.shape[1],
            bytes_accessed=2 * down.shape[0] * down.shape[1],
            transcendentals=0,
        ),
        name="shared_out",
    )(branch, down, *acts)


def narrow_sum(keep, send):
    return chip_sum(keep + core_swap(send).astype(jnp.float32))


def chip_sum(total):
    chips = lax.axis_size("narrow") // 2
    part = total.shape[0] // chips
    result = total[:part]
    for d in range(1, chips):
        piece = total[d * part : (d + 1) * part].astype(jnp.bfloat16)
        result = result + x_shift(piece, -d).astype(jnp.float32)
    return result


def body(
    tokens,
    expert_ids,
    route_weights,
    expert_gate,
    expert_up,
    expert_down,
    shared_gate,
    shared_up,
    shared_down,
    shared_scale,
):
    rows, feat = tokens.shape
    spread = lax.axis_size("expert")
    here = lax.axis_index("expert")
    local = expert_gate.shape[0]
    depth = shared_gate.shape[0]
    chosen = expert_ids.shape[1]
    own = jnp.concatenate(
        [
            tokens,
            expert_ids.astype(jnp.bfloat16),
            route_weights,
            jnp.zeros((rows, LANES - 2 * chosen), jnp.bfloat16),
        ],
        axis=1,
    )
    column = jnp.concatenate(gather_column([own] * spread), axis=0)
    part = lax.dynamic_slice_in_dim(column, here * depth, depth, axis=1)
    parts, (column,), up = join(gather_plane(part), [column], load([shared_up], shared_up.shape[0]))
    parts = parts + [core_swap(piece) for piece in parts]
    hidden_own, *hidden_parts = shared_in(parts, shared_gate, *up, rows)
    plane, (hidden_own,) = join(gather_plane(column), [hidden_own])
    x = both_cores(jnp.concatenate(plane, axis=0))

    first = (here * local).astype(jnp.int32).reshape(1)
    branch, keep, send = experts(
        x, shared_scale, expert_gate, expert_up, expert_down, first, chosen
    )
    arrived = [z_shift(piece, -d) for d, piece in enumerate(hidden_parts, 1)]
    arrived, (keep, send) = join(arrived, [keep, send])
    hidden = hidden_own.astype(jnp.float32)
    for piece in arrived:
        hidden = hidden + piece.astype(jnp.float32)
    shared_act = (jax.nn.silu(hidden[0]) * hidden[1]).astype(jnp.bfloat16)
    acts = gather_column([shared_act] * spread)
    routed = keep + core_swap(send).astype(jnp.float32)
    middle = feat // LANES // 2 * LANES
    routed = [chip_sum(routed[:, :middle]), chip_sum(routed[:, middle:])]
    down = join([shared_down, shared_act])[0][:1]
    acts, down = join(acts, load(down, shared_down.shape[0]))
    part = shared_out(branch, *down, acts, rows)
    part, routed = join(part, routed)
    both = jnp.concatenate([*routed, narrow_sum(*part)], axis=1)
    pieces = [both[:rows]] + [
        z_shift(both[d * rows : (d + 1) * rows].astype(jnp.bfloat16), -d).astype(jnp.float32)
        for d in range(1, spread)
    ]
    total = pieces[0][:, :feat]
    for piece in pieces[1:]:
        total = total + piece[:, :feat]
    width = shared_down.shape[1]
    for d, piece in enumerate(pieces):
        at = lax.rem(here + d, spread) * width
        old = lax.dynamic_slice_in_dim(total, at, width, axis=1)
        total = lax.dynamic_update_slice_in_dim(total, old + piece[:, feat:], at, axis=1)
    return total.astype(jnp.bfloat16)


def solution(mesh):
    return jax.shard_map(
        body,
        mesh=mesh,
        in_specs=(
            P(("groups", "expert", "narrow"), None),
            P(("groups", "expert", "narrow"), None),
            P(("groups", "expert", "narrow"), None),
            P("expert", None, "narrow"),
            P("expert", None, "narrow"),
            P("expert", "narrow", None),
            P("expert", "narrow"),
            P("expert", "narrow"),
            P("narrow", "expert"),
            P(),
        ),
        out_specs=P(("groups", "expert", "narrow"), None),
        check_vma=False,
    )
```

```python
import functools
import math

import jax
import jax.numpy as jnp
from jax import lax
from jax.experimental import pallas as pl
from jax.experimental.pallas import tpu as pltpu
from jax.sharding import PartitionSpec as P

EXPERTS = 32
LANES = 128
VMEM_LIMIT = 48 * 2**20
VMEM_SMALL = 8 * 2**20


def chunk_of(width, most):
    best = width
    for size in range(LANES, most + 1, LANES):
        if width % size == 0:
            best = size
    return best


def z_shift(value, step):
    spread = lax.axis_size("expert")
    return lax.ppermute(value, "expert", [(i, (i + step) % spread) for i in range(spread)])


def x_shift(value, step):
    size = lax.axis_size("narrow")
    return lax.ppermute(value, "narrow", [(i, (i + 2 * step) % size) for i in range(size)])


def core_swap(value):
    size = lax.axis_size("narrow")
    return lax.ppermute(value, "narrow", [(i, i ^ 1) for i in range(size)])


def gather_column(pieces):
    return [pieces[0]] + [z_shift(piece, d) for d, piece in enumerate(pieces) if d > 0]


def gather_plane(column):
    chips = lax.axis_size("narrow") // 2
    return [column] + [x_shift(column, d) for d in range(1, chips)]


def both_cores(plane):
    return jnp.concatenate([plane, core_swap(plane)], axis=0)


def join(*lists):
    values = iter(lax.optimization_barrier([value for part in lists for value in part]))
    return [[next(values) for _ in part] for part in lists]


def load_kernel(*refs):
    count = len(refs) // 2
    sources, targets, sems = refs[:count], refs[count:-1], refs[-1]
    copies = [
        pltpu.make_async_copy(source.at[pl.ds(0, target.shape[0])], target, sems.at[i])
        for i, (source, target) in enumerate(zip(sources, targets))
    ]
    for copy in copies:
        copy.start()
    for copy in copies:
        copy.wait()


def load(arrays, taken):
    shapes = [(taken, *value.shape[1:]) for value in arrays]
    return pl.pallas_call(
        load_kernel,
        in_specs=[pl.BlockSpec(memory_space=pl.ANY)] * len(arrays),
        out_shape=[
            jax.ShapeDtypeStruct(shape, value.dtype) for shape, value in zip(shapes, arrays)
        ],
        scratch_shapes=[pltpu.SemaphoreType.DMA((len(arrays),))],
        compiler_params=pltpu.CompilerParams(vmem_limit_bytes=VMEM_SMALL),
        cost_estimate=pl.CostEstimate(
            flops=0,
            bytes_accessed=sum(2 * math.prod(shape) for shape in shapes),
            transcendentals=0,
        ),
        name="load",
    )(*arrays)


def shared_in_kernel(sizes, width, gate_ref, up_ref, *refs):
    outer, spread, rows = sizes
    x_refs, out_refs = refs[:outer], refs[outer : outer + spread]
    x_buf, sems = refs[outer + spread :]
    copies = [
        pltpu.make_async_copy(ref, x_buf.at[i], sems.at[i]) for i, ref in enumerate(x_refs)
    ]
    for copy in copies:
        copy.start()
    for copy in copies:
        copy.wait()
    x = x_buf[...].reshape(outer * spread * rows, x_buf.shape[2])
    for half, ref in enumerate((gate_ref, up_ref)):
        for j in range(ref.shape[1] // width):
            columns = pl.ds(j * width, width)
            sums = jnp.dot(x, ref[:, columns], preferred_element_type=jnp.float32)
            sums = sums.reshape(outer, spread, rows, width)
            for d in range(spread):
                block = sums[:, d].reshape(outer * rows, width)
                out_refs[d][half, :, columns] = block.astype(jnp.bfloat16)


def shared_in(pieces, gate, up, rows):
    depth, hidden = gate.shape
    outer, spread = len(pieces), lax.axis_size("expert")
    count = outer * spread * rows
    whole = pl.BlockSpec(memory_space=pltpu.VMEM)
    apart = pl.BlockSpec(memory_space=pl.ANY)
    return pl.pallas_call(
        functools.partial(shared_in_kernel, (outer, spread, rows), chunk_of(hidden, 512)),
        in_specs=[whole, whole] + [apart] * outer,
        out_shape=[jax.ShapeDtypeStruct((2, outer * rows, hidden), jnp.bfloat16)] * spread,
        scratch_shapes=[
            pltpu.VMEM((outer, spread * rows, depth), gate.dtype),
            pltpu.SemaphoreType.DMA((outer,)),
        ],
        compiler_params=pltpu.CompilerParams(vmem_limit_bytes=VMEM_SMALL),
        cost_estimate=pl.CostEstimate(
            flops=4 * count * depth * hidden,
            bytes_accessed=4 * count * hidden,
            transcendentals=0,
        ),
        name="shared_in",
    )(gate, up, *pieces)


def experts_kernel(chosen, first_ref, x_ref, scale_ref, gate_ref, up_ref, down_ref, *refs):
    branch_ref, keep_ref, send_ref = refs[:3]
    act_buf, gate_buf, up_buf, down_buf, sems, down_sems = refs[3:]
    local, feat, hidden = gate_ref.shape
    slots, (down_slots, _, _, width) = gate_buf.shape[0], down_buf.shape
    blocks = feat // width

    def copies(i):
        slot = i % slots
        return [
            pltpu.make_async_copy(ref.at[i], buf.at[slot], sems.at[half, slot])
            for half, (ref, buf) in enumerate(((gate_ref, gate_buf), (up_ref, up_buf)))
        ]

    def down_copy(j):
        slot = j % down_slots
        return pltpu.make_async_copy(
            down_ref.at[:, :, pl.ds(j * width, width)], down_buf.at[slot], down_sems.at[slot]
        )

    for i in range(slots):
        for copy in copies(i):
            copy.start()
    inner = jnp.sum(x_ref[:, :feat].astype(jnp.float32) * scale_ref[...], axis=1, keepdims=True)
    branch_ref[...] = jnp.broadcast_to(1.0 / (1.0 + jnp.exp(-inner)), branch_ref.shape)
    route = x_ref[:, feat:].astype(jnp.float32)
    named, weights = route[:, :chosen], route[:, chosen : 2 * chosen]
    x = x_ref[:, :feat]
    for i in range(local):
        slot = i % slots
        gate_copy, up_copy = copies(i)
        gate_copy.wait()
        gate = jnp.dot(x, gate_buf[slot], preferred_element_type=jnp.float32)
        up_copy.wait()
        up = jnp.dot(x, up_buf[slot], preferred_element_type=jnp.float32)
        if i + slots < local:
            for copy in copies(i + slots):
                copy.start()
        if i == max(local - slots, 0):
            for j in range(down_slots):
                down_copy(j).start()
        expert = (first_ref[0] + i).astype(jnp.float32)
        weight = jnp.sum(jnp.where(named == expert, weights, 0.0), axis=1, keepdims=True)
        value = gate / (1.0 + jnp.exp(-gate)) * up * weight
        act_buf[:, i * hidden : (i + 1) * hidden] = jnp.where(
            weight == 0.0, 0.0, value
        ).astype(jnp.bfloat16)
    half = act_buf.shape[0] // 2
    for j in range(blocks):
        down_copy(j).wait()
        sums = jnp.dot(
            act_buf[...],
            down_buf[j % down_slots].reshape(local * hidden, width),
            preferred_element_type=jnp.float32,
        )
        if j + down_slots < blocks:
            down_copy(j + down_slots).start()
        at = pl.ds(j * width, width)
        keep_ref[:, at] = sums[:half]
        send_ref[:, at] = sums[half:].astype(jnp.bfloat16)


def experts(x, scale, gate, up, down, first, chosen):
    count = x.shape[0]
    local, feat, hidden = gate.shape
    whole = pl.BlockSpec(memory_space=pltpu.VMEM)
    apart = pl.BlockSpec(memory_space=pl.ANY)
    slots = min(3, local)
    width = chunk_of(feat, 256)
    down_slots = (feat // width + 1) // 2
    buffer = pltpu.VMEM((slots, feat, hidden), gate.dtype)
    return pl.pallas_call(
        functools.partial(experts_kernel, chosen),
        in_specs=[pl.BlockSpec(memory_space=pltpu.SMEM), whole, whole, apart, apart, apart],
        out_shape=[
            jax.ShapeDtypeStruct((count, LANES), jnp.float32),
            jax.ShapeDtypeStruct((count // 2, feat), jnp.float32),
            jax.ShapeDtypeStruct((count // 2, feat), jnp.bfloat16),
        ],
        scratch_shapes=[
            pltpu.VMEM((count, local * hidden), jnp.bfloat16),
            buffer,
            buffer,
            pltpu.VMEM((down_slots, local, hidden, width), down.dtype),
            pltpu.SemaphoreType.DMA((2, slots)),
            pltpu.SemaphoreType.DMA((down_slots,)),
        ],
        compiler_params=pltpu.CompilerParams(vmem_limit_bytes=VMEM_LIMIT),
        cost_estimate=pl.CostEstimate(
            flops=6 * count * local * feat * hidden,
            bytes_accessed=6 * local * feat * hidden,
            transcendentals=count * local * hidden,
        ),
        name="experts",
    )(first, x, scale.reshape(1, feat), gate, up, down)


def shared_out_kernel(sizes, branch_ref, down_ref, *refs):
    outer, spread, rows = sizes
    act_refs, (keep_ref, send_ref) = refs[:spread], refs[spread:]
    act = jnp.concatenate([ref[...] for ref in act_refs], axis=0)
    sums = jnp.dot(act, down_ref[...], preferred_element_type=jnp.float32)
    width = sums.shape[1]
    sums = jnp.swapaxes(sums.reshape(spread, outer, rows, width), 0, 1)
    sums = sums.reshape(outer * spread * rows, width) * branch_ref[:, :1]
    half = sums.shape[0] // 2
    keep_ref[...] = sums[:half]
    send_ref[...] = sums[half:].astype(jnp.bfloat16)


def shared_out(branch, down, acts, rows):
    count, spread = branch.shape[0], len(acts)
    outer = count // (spread * rows)
    shape = (count // 2, down.shape[1])
    return pl.pallas_call(
        functools.partial(shared_out_kernel, (outer, spread, rows)),
        out_shape=[
            jax.ShapeDtypeStruct(shape, jnp.float32),
            jax.ShapeDtypeStruct(shape, jnp.bfloat16),
        ],
        compiler_params=pltpu.CompilerParams(vmem_limit_bytes=VMEM_LIMIT),
        cost_estimate=pl.CostEstimate(
            flops=2 * count * down.shape[0] * down.shape[1],
            bytes_accessed=2 * down.shape[0] * down.shape[1],
            transcendentals=0,
        ),
        name="shared_out",
    )(branch, down, *acts)


def narrow_sum(keep, send):
    return chip_sum(keep + core_swap(send).astype(jnp.float32))


def chip_sum(total):
    chips = lax.axis_size("narrow") // 2
    part = total.shape[0] // chips
    result = total[:part]
    for d in range(1, chips):
        piece = total[d * part : (d + 1) * part].astype(jnp.bfloat16)
        result = result + x_shift(piece, -d).astype(jnp.float32)
    return result


def body(
    tokens,
    expert_ids,
    route_weights,
    expert_gate,
    expert_up,
    expert_down,
    shared_gate,
    shared_up,
    shared_down,
    shared_scale,
):
    rows, feat = tokens.shape
    spread = lax.axis_size("expert")
    here = lax.axis_index("expert")
    local = expert_gate.shape[0]
    depth = shared_gate.shape[0]
    chosen = expert_ids.shape[1]
    own = jnp.concatenate(
        [
            tokens,
            expert_ids.astype(jnp.bfloat16),
            route_weights,
            jnp.zeros((rows, LANES - 2 * chosen), jnp.bfloat16),
        ],
        axis=1,
    )
    column = jnp.concatenate(gather_column([own] * spread), axis=0)
    part = lax.dynamic_slice_in_dim(column, here * depth, depth, axis=1)
    early = jnp.concatenate([part, column[:, feat:]], axis=1)
    early, up = join(gather_plane(early), load([shared_up], shared_up.shape[0]))
    parts = [piece[:, :depth] for piece in early]
    parts = parts + [core_swap(piece) for piece in parts]
    hidden_own, *hidden_parts = shared_in(parts, shared_gate, *up, rows)
    plane, (hidden_own,) = join(gather_plane(column[:, :feat]), [hidden_own])
    plane = [
        jnp.concatenate([piece, rest[:, depth:]], axis=1) for piece, rest in zip(plane, early)
    ]
    x = both_cores(jnp.concatenate(plane, axis=0))

    first = (here * local).astype(jnp.int32).reshape(1)
    branch, keep, send = experts(
        x, shared_scale, expert_gate, expert_up, expert_down, first, chosen
    )
    arrived = [z_shift(piece, -d) for d, piece in enumerate(hidden_parts, 1)]
    arrived, (keep, send) = join(arrived, [keep, send])
    hidden = hidden_own.astype(jnp.float32)
    for piece in arrived:
        hidden = hidden + piece.astype(jnp.float32)
    shared_act = (jax.nn.silu(hidden[0]) * hidden[1]).astype(jnp.bfloat16)
    acts = gather_column([shared_act] * spread)
    routed = keep + core_swap(send).astype(jnp.float32)
    middle = feat // LANES // 2 * LANES
    routed = [chip_sum(routed[:, :middle]), chip_sum(routed[:, middle:])]
    down = join([shared_down, shared_act])[0][:1]
    acts, down = join(acts, load(down, shared_down.shape[0]))
    part = shared_out(branch, *down, acts, rows)
    part, routed = join(part, routed)
    both = jnp.concatenate([*routed, narrow_sum(*part)], axis=1)
    pieces = [both[:rows]] + [
        z_shift(both[d * rows : (d + 1) * rows].astype(jnp.bfloat16), -d).astype(jnp.float32)
        for d in range(1, spread)
    ]
    total = pieces[0][:, :feat]
    for piece in pieces[1:]:
        total = total + piece[:, :feat]
    width = shared_down.shape[1]
    for d, piece in enumerate(pieces):
        at = lax.rem(here + d, spread) * width
        old = lax.dynamic_slice_in_dim(total, at, width, axis=1)
        total = lax.dynamic_update_slice_in_dim(total, old + piece[:, feat:], at, axis=1)
    return total.astype(jnp.bfloat16)


def solution(mesh):
    return jax.shard_map(
        body,
        mesh=mesh,
        in_specs=(
            P(("groups", "expert", "narrow"), None),
            P(("groups", "expert", "narrow"), None),
            P(("groups", "expert", "narrow"), None),
            P("expert", None, "narrow"),
            P("expert", None, "narrow"),
            P("expert", "narrow", None),
            P("expert", "narrow"),
            P("expert", "narrow"),
            P("narrow", "expert"),
            P(),
        ),
        out_specs=P(("groups", "expert", "narrow"), None),
        check_vma=False,
    )
```

```python
import functools
import math

import jax
import jax.numpy as jnp
from jax import lax
from jax.experimental import pallas as pl
from jax.experimental.pallas import tpu as pltpu
from jax.sharding import PartitionSpec as P

EXPERTS = 32
LANES = 128
VMEM_LIMIT = 48 * 2**20
VMEM_SMALL = 8 * 2**20


def chunk_of(width, most):
    best = width
    for size in range(LANES, most + 1, LANES):
        if width % size == 0:
            best = size
    return best


def z_shift(value, step):
    spread = lax.axis_size("expert")
    return lax.ppermute(value, "expert", [(i, (i + step) % spread) for i in range(spread)])


def x_shift(value, step):
    size = lax.axis_size("narrow")
    return lax.ppermute(value, "narrow", [(i, (i + 2 * step) % size) for i in range(size)])


def core_swap(value):
    size = lax.axis_size("narrow")
    return lax.ppermute(value, "narrow", [(i, i ^ 1) for i in range(size)])


def gather_column(pieces):
    return [pieces[0]] + [z_shift(piece, d) for d, piece in enumerate(pieces) if d > 0]


def gather_plane(column):
    chips = lax.axis_size("narrow") // 2
    return [column] + [x_shift(column, d) for d in range(1, chips)]


def both_cores(plane):
    return jnp.concatenate([plane, core_swap(plane)], axis=0)


def join(*lists):
    values = iter(lax.optimization_barrier([value for part in lists for value in part]))
    return [[next(values) for _ in part] for part in lists]


def load_kernel(*refs):
    count = len(refs) // 2
    sources, targets, sems = refs[:count], refs[count:-1], refs[-1]
    copies = [
        pltpu.make_async_copy(source.at[pl.ds(0, target.shape[0])], target, sems.at[i])
        for i, (source, target) in enumerate(zip(sources, targets))
    ]
    for copy in copies:
        copy.start()
    for copy in copies:
        copy.wait()


def load(arrays, taken):
    shapes = [(taken, *value.shape[1:]) for value in arrays]
    return pl.pallas_call(
        load_kernel,
        in_specs=[pl.BlockSpec(memory_space=pl.ANY)] * len(arrays),
        out_shape=[
            jax.ShapeDtypeStruct(shape, value.dtype) for shape, value in zip(shapes, arrays)
        ],
        scratch_shapes=[pltpu.SemaphoreType.DMA((len(arrays),))],
        compiler_params=pltpu.CompilerParams(vmem_limit_bytes=VMEM_SMALL),
        cost_estimate=pl.CostEstimate(
            flops=0,
            bytes_accessed=sum(2 * math.prod(shape) for shape in shapes),
            transcendentals=0,
        ),
        name="load",
    )(*arrays)


def shared_in_kernel(sizes, width, gate_ref, up_ref, *refs):
    outer, spread, rows = sizes
    x_refs, out_refs = refs[:outer], refs[outer : outer + spread]
    x_buf, sems = refs[outer + spread :]
    copies = [
        pltpu.make_async_copy(ref, x_buf.at[i], sems.at[i]) for i, ref in enumerate(x_refs)
    ]
    for copy in copies:
        copy.start()
    for copy in copies:
        copy.wait()
    x = x_buf[...].reshape(outer * spread * rows, x_buf.shape[2])
    for half, ref in enumerate((gate_ref, up_ref)):
        for j in range(ref.shape[1] // width):
            columns = pl.ds(j * width, width)
            sums = jnp.dot(x, ref[:, columns], preferred_element_type=jnp.float32)
            sums = sums.reshape(outer, spread, rows, width)
            for d in range(spread):
                block = sums[:, d].reshape(outer * rows, width)
                out_refs[d][half, :, columns] = block.astype(jnp.bfloat16)


def shared_in(pieces, gate, up, rows):
    depth, hidden = gate.shape
    outer, spread = len(pieces), lax.axis_size("expert")
    count = outer * spread * rows
    whole = pl.BlockSpec(memory_space=pltpu.VMEM)
    apart = pl.BlockSpec(memory_space=pl.ANY)
    return pl.pallas_call(
        functools.partial(shared_in_kernel, (outer, spread, rows), chunk_of(hidden, 512)),
        in_specs=[whole, whole] + [apart] * outer,
        out_shape=[jax.ShapeDtypeStruct((2, outer * rows, hidden), jnp.bfloat16)] * spread,
        scratch_shapes=[
            pltpu.VMEM((outer, spread * rows, depth), gate.dtype),
            pltpu.SemaphoreType.DMA((outer,)),
        ],
        compiler_params=pltpu.CompilerParams(vmem_limit_bytes=VMEM_SMALL),
        cost_estimate=pl.CostEstimate(
            flops=4 * count * depth * hidden,
            bytes_accessed=4 * count * hidden,
            transcendentals=0,
        ),
        name="shared_in",
    )(gate, up, *pieces)


def experts_kernel(chosen, first_ref, x_ref, scale_ref, gate_ref, up_ref, down_ref, *refs):
    branch_ref, keep_ref, send_ref = refs[:3]
    act_buf, gate_buf, up_buf, down_buf, sems, down_sems = refs[3:]
    local, feat, hidden = gate_ref.shape
    slots, (down_slots, _, _, width) = gate_buf.shape[0], down_buf.shape
    blocks = feat // width

    def copies(i):
        slot = i % slots
        return [
            pltpu.make_async_copy(ref.at[i], buf.at[slot], sems.at[half, slot])
            for half, (ref, buf) in enumerate(((gate_ref, gate_buf), (up_ref, up_buf)))
        ]

    def down_copy(j):
        slot = j % down_slots
        return pltpu.make_async_copy(
            down_ref.at[:, :, pl.ds(j * width, width)], down_buf.at[slot], down_sems.at[slot]
        )

    for i in range(slots):
        for copy in copies(i):
            copy.start()
    inner = jnp.sum(x_ref[:, :feat].astype(jnp.float32) * scale_ref[...], axis=1, keepdims=True)
    branch_ref[...] = jnp.broadcast_to(1.0 / (1.0 + jnp.exp(-inner)), branch_ref.shape)
    route = x_ref[:, feat:].astype(jnp.float32)
    named, weights = route[:, :chosen], route[:, chosen : 2 * chosen]
    x = x_ref[:, :feat]
    for i in range(local):
        slot = i % slots
        gate_copy, up_copy = copies(i)
        gate_copy.wait()
        gate = jnp.dot(x, gate_buf[slot], preferred_element_type=jnp.float32)
        up_copy.wait()
        up = jnp.dot(x, up_buf[slot], preferred_element_type=jnp.float32)
        if i + slots < local:
            for copy in copies(i + slots):
                copy.start()
        if i == max(local - slots, 0):
            for j in range(down_slots):
                down_copy(j).start()
        expert = (first_ref[0] + i).astype(jnp.float32)
        weight = jnp.sum(jnp.where(named == expert, weights, 0.0), axis=1, keepdims=True)
        value = gate / (1.0 + jnp.exp(-gate)) * up * weight
        act_buf[:, i * hidden : (i + 1) * hidden] = jnp.where(
            weight == 0.0, 0.0, value
        ).astype(jnp.bfloat16)
    half = act_buf.shape[0] // 2
    for j in range(blocks):
        down_copy(j).wait()
        sums = jnp.dot(
            act_buf[...],
            down_buf[j % down_slots].reshape(local * hidden, width),
            preferred_element_type=jnp.float32,
        )
        if j + down_slots < blocks:
            down_copy(j + down_slots).start()
        at = pl.ds(j * width, width)
        keep_ref[:, at] = sums[:half]
        send_ref[:, at] = sums[half:].astype(jnp.bfloat16)


def experts(x, scale, gate, up, down, first, chosen):
    count = x.shape[0]
    local, feat, hidden = gate.shape
    whole = pl.BlockSpec(memory_space=pltpu.VMEM)
    apart = pl.BlockSpec(memory_space=pl.ANY)
    slots = min(3, local)
    width = chunk_of(feat, 256)
    down_slots = (feat // width + 1) // 2
    buffer = pltpu.VMEM((slots, feat, hidden), gate.dtype)
    return pl.pallas_call(
        functools.partial(experts_kernel, chosen),
        in_specs=[pl.BlockSpec(memory_space=pltpu.SMEM), whole, whole, apart, apart, apart],
        out_shape=[
            jax.ShapeDtypeStruct((count, LANES), jnp.float32),
            jax.ShapeDtypeStruct((count // 2, feat), jnp.float32),
            jax.ShapeDtypeStruct((count // 2, feat), jnp.bfloat16),
        ],
        scratch_shapes=[
            pltpu.VMEM((count, local * hidden), jnp.bfloat16),
            buffer,
            buffer,
            pltpu.VMEM((down_slots, local, hidden, width), down.dtype),
            pltpu.SemaphoreType.DMA((2, slots)),
            pltpu.SemaphoreType.DMA((down_slots,)),
        ],
        compiler_params=pltpu.CompilerParams(vmem_limit_bytes=VMEM_LIMIT),
        cost_estimate=pl.CostEstimate(
            flops=6 * count * local * feat * hidden,
            bytes_accessed=6 * local * feat * hidden,
            transcendentals=count * local * hidden,
        ),
        name="experts",
    )(first, x, scale.reshape(1, feat), gate, up, down)


def shared_out_kernel(sizes, branch_ref, down_ref, *refs):
    outer, spread, rows = sizes
    act_refs, (keep_ref, send_ref) = refs[:spread], refs[spread:]
    act = jnp.concatenate([ref[...] for ref in act_refs], axis=0)
    sums = jnp.dot(act, down_ref[...], preferred_element_type=jnp.float32)
    width = sums.shape[1]
    sums = jnp.swapaxes(sums.reshape(spread, outer, rows, width), 0, 1)
    sums = sums.reshape(outer * spread * rows, width) * branch_ref[:, :1]
    half = sums.shape[0] // 2
    keep_ref[...] = sums[:half]
    send_ref[...] = sums[half:].astype(jnp.bfloat16)


def shared_out(branch, down, acts, rows):
    count, spread = branch.shape[0], len(acts)
    outer = count // (spread * rows)
    shape = (count // 2, down.shape[1])
    return pl.pallas_call(
        functools.partial(shared_out_kernel, (outer, spread, rows)),
        out_shape=[
            jax.ShapeDtypeStruct(shape, jnp.float32),
            jax.ShapeDtypeStruct(shape, jnp.bfloat16),
        ],
        compiler_params=pltpu.CompilerParams(vmem_limit_bytes=VMEM_LIMIT),
        cost_estimate=pl.CostEstimate(
            flops=2 * count * down.shape[0] * down.shape[1],
            bytes_accessed=2 * down.shape[0] * down.shape[1],
            transcendentals=0,
        ),
        name="shared_out",
    )(branch, down, *acts)


def narrow_sum(keep, send):
    return chip_sum(keep + core_swap(send).astype(jnp.float32))


def chip_sum(total):
    chips = lax.axis_size("narrow") // 2
    part = total.shape[0] // chips
    result = total[:part]
    for d in range(1, chips):
        piece = total[d * part : (d + 1) * part].astype(jnp.bfloat16)
        result = result + x_shift(piece, -d).astype(jnp.float32)
    return result


def body(
    tokens,
    expert_ids,
    route_weights,
    expert_gate,
    expert_up,
    expert_down,
    shared_gate,
    shared_up,
    shared_down,
    shared_scale,
):
    rows, feat = tokens.shape
    spread = lax.axis_size("expert")
    here = lax.axis_index("expert")
    local = expert_gate.shape[0]
    depth = shared_gate.shape[0]
    chosen = expert_ids.shape[1]
    own = jnp.concatenate(
        [
            tokens,
            expert_ids.astype(jnp.bfloat16),
            route_weights,
            jnp.zeros((rows, LANES - 2 * chosen), jnp.bfloat16),
        ],
        axis=1,
    )
    column = jnp.concatenate(gather_column([own] * spread), axis=0)
    part = lax.dynamic_slice_in_dim(column, here * depth, depth, axis=1)
    early = jnp.concatenate([part, column[:, feat:]], axis=1)
    early, up = join(gather_plane(early), load([shared_up], shared_up.shape[0]))
    parts = [piece[:, :depth] for piece in early]
    parts = parts + [core_swap(piece) for piece in parts]
    hidden_own, *hidden_parts = shared_in(parts, shared_gate, *up, rows)
    plane, (hidden_own,) = join(gather_plane(column[:, :feat]), [hidden_own])
    plane = [
        jnp.concatenate([piece, rest[:, depth:]], axis=1) for piece, rest in zip(plane, early)
    ]
    x = both_cores(jnp.concatenate(plane, axis=0))

    first = (here * local).astype(jnp.int32).reshape(1)
    branch, keep, send = experts(
        x, shared_scale, expert_gate, expert_up, expert_down, first, chosen
    )
    arrived = [z_shift(piece, -d) for d, piece in enumerate(hidden_parts, 1)]
    arrived, (keep, send) = join(arrived, [keep, send])
    hidden = hidden_own.astype(jnp.float32)
    for piece in arrived:
        hidden = hidden + piece.astype(jnp.float32)
    shared_act = (jax.nn.silu(hidden[0]) * hidden[1]).astype(jnp.bfloat16)
    acts = gather_column([shared_act] * spread)
    routed = keep + core_swap(send).astype(jnp.float32)
    middle = feat // LANES // 2 * LANES
    routed = [chip_sum(routed[:, :middle]), chip_sum(routed[:, middle:])]
    down = join([shared_down, shared_act])[0][:1]
    acts, down = join(acts, load(down, shared_down.shape[0]))
    part = shared_out(branch, *down, acts, rows)
    part, routed = join(part, routed)
    total, part = jnp.concatenate(routed, axis=1), narrow_sum(*part)
    at = here * part.shape[1]
    part = part + lax.dynamic_slice_in_dim(total, at, part.shape[1], axis=1)
    total = lax.dynamic_update_slice_in_dim(total, part, at, axis=1)
    out = total[:rows]
    for d in range(1, spread):
        piece = total[d * rows : (d + 1) * rows].astype(jnp.bfloat16)
        out = out + z_shift(piece, -d).astype(jnp.float32)
    return out.astype(jnp.bfloat16)


def solution(mesh):
    return jax.shard_map(
        body,
        mesh=mesh,
        in_specs=(
            P(("groups", "expert", "narrow"), None),
            P(("groups", "expert", "narrow"), None),
            P(("groups", "expert", "narrow"), None),
            P("expert", None, "narrow"),
            P("expert", None, "narrow"),
            P("expert", "narrow", None),
            P("expert", "narrow"),
            P("expert", "narrow"),
            P("narrow", "expert"),
            P(),
        ),
        out_specs=P(("groups", "expert", "narrow"), None),
        check_vma=False,
    )
```

```python
import functools
import math

import jax
import jax.numpy as jnp
from jax import lax
from jax.experimental import pallas as pl
from jax.experimental.pallas import tpu as pltpu
from jax.sharding import PartitionSpec as P

EXPERTS = 32
LANES = 128
VMEM_LIMIT = 48 * 2**20
VMEM_SMALL = 8 * 2**20


def chunk_of(width, most):
    best = width
    for size in range(LANES, most + 1, LANES):
        if width % size == 0:
            best = size
    return best


def z_shift(value, step):
    spread = lax.axis_size("expert")
    return lax.ppermute(value, "expert", [(i, (i + step) % spread) for i in range(spread)])


def x_shift(value, step):
    size = lax.axis_size("narrow")
    return lax.ppermute(value, "narrow", [(i, (i + 2 * step) % size) for i in range(size)])


def core_swap(value):
    size = lax.axis_size("narrow")
    return lax.ppermute(value, "narrow", [(i, i ^ 1) for i in range(size)])


def gather_column(pieces):
    return [pieces[0]] + [z_shift(piece, d) for d, piece in enumerate(pieces) if d > 0]


def gather_plane(column):
    chips = lax.axis_size("narrow") // 2
    return [column] + [x_shift(column, d) for d in range(1, chips)]


def both_cores(plane):
    return jnp.concatenate([plane, core_swap(plane)], axis=0)


def join(*lists):
    values = iter(lax.optimization_barrier([value for part in lists for value in part]))
    return [[next(values) for _ in part] for part in lists]


def load_kernel(*refs):
    count = len(refs) // 2
    sources, targets, sems = refs[:count], refs[count:-1], refs[-1]
    copies = [
        pltpu.make_async_copy(source.at[pl.ds(0, target.shape[0])], target, sems.at[i])
        for i, (source, target) in enumerate(zip(sources, targets))
    ]
    for copy in copies:
        copy.start()
    for copy in copies:
        copy.wait()


def load(arrays, taken):
    shapes = [(taken, *value.shape[1:]) for value in arrays]
    return pl.pallas_call(
        load_kernel,
        in_specs=[pl.BlockSpec(memory_space=pl.ANY)] * len(arrays),
        out_shape=[
            jax.ShapeDtypeStruct(shape, value.dtype) for shape, value in zip(shapes, arrays)
        ],
        scratch_shapes=[pltpu.SemaphoreType.DMA((len(arrays),))],
        compiler_params=pltpu.CompilerParams(vmem_limit_bytes=VMEM_SMALL),
        cost_estimate=pl.CostEstimate(
            flops=0,
            bytes_accessed=sum(2 * math.prod(shape) for shape in shapes),
            transcendentals=0,
        ),
        name="load",
    )(*arrays)


def shared_in_kernel(sizes, width, gate_ref, up_ref, *refs):
    outer, spread, rows = sizes
    x_refs, out_refs = refs[:outer], refs[outer : outer + spread]
    x_buf, sems = refs[outer + spread :]
    copies = [
        pltpu.make_async_copy(ref, x_buf.at[i], sems.at[i]) for i, ref in enumerate(x_refs)
    ]
    for copy in copies:
        copy.start()
    for copy in copies:
        copy.wait()
    x = x_buf[...].reshape(outer * spread * rows, x_buf.shape[2])
    for half, ref in enumerate((gate_ref, up_ref)):
        for j in range(ref.shape[1] // width):
            columns = pl.ds(j * width, width)
            sums = jnp.dot(x, ref[:, columns], preferred_element_type=jnp.float32)
            sums = sums.reshape(outer, spread, rows, width)
            for d in range(spread):
                block = sums[:, d].reshape(outer * rows, width)
                out_refs[d][half, :, columns] = block.astype(jnp.bfloat16)


def shared_in(pieces, gate, up, rows):
    depth, hidden = gate.shape
    outer, spread = len(pieces), lax.axis_size("expert")
    count = outer * spread * rows
    whole = pl.BlockSpec(memory_space=pltpu.VMEM)
    apart = pl.BlockSpec(memory_space=pl.ANY)
    return pl.pallas_call(
        functools.partial(shared_in_kernel, (outer, spread, rows), chunk_of(hidden, 512)),
        in_specs=[whole, whole] + [apart] * outer,
        out_shape=[jax.ShapeDtypeStruct((2, outer * rows, hidden), jnp.bfloat16)] * spread,
        scratch_shapes=[
            pltpu.VMEM((outer, spread * rows, depth), gate.dtype),
            pltpu.SemaphoreType.DMA((outer,)),
        ],
        compiler_params=pltpu.CompilerParams(vmem_limit_bytes=VMEM_SMALL),
        cost_estimate=pl.CostEstimate(
            flops=4 * count * depth * hidden,
            bytes_accessed=4 * count * hidden,
            transcendentals=0,
        ),
        name="shared_in",
    )(gate, up, *pieces)


def experts_kernel(chosen, first_ref, x_ref, scale_ref, gate_ref, up_ref, down_ref, *refs):
    branch_ref, keep_ref, send_ref = refs[:3]
    act_buf, gate_buf, up_buf, down_buf, sems, down_sems = refs[3:]
    local, feat, hidden = gate_ref.shape
    slots, (down_slots, _, _, width) = gate_buf.shape[0], down_buf.shape
    blocks = feat // width

    def copies(i):
        slot = i % slots
        return [
            pltpu.make_async_copy(ref.at[i], buf.at[slot], sems.at[half, slot])
            for half, (ref, buf) in enumerate(((gate_ref, gate_buf), (up_ref, up_buf)))
        ]

    def down_copy(j):
        slot = j % down_slots
        return pltpu.make_async_copy(
            down_ref.at[:, :, pl.ds(j * width, width)], down_buf.at[slot], down_sems.at[slot]
        )

    for i in range(slots):
        for copy in copies(i):
            copy.start()
    inner = jnp.sum(x_ref[:, :feat].astype(jnp.float32) * scale_ref[...], axis=1, keepdims=True)
    branch_ref[...] = jnp.broadcast_to(1.0 / (1.0 + jnp.exp(-inner)), branch_ref.shape)
    route = x_ref[:, feat:].astype(jnp.float32)
    named, weights = route[:, :chosen], route[:, chosen : 2 * chosen]
    x = x_ref[:, :feat]
    for i in range(local):
        slot = i % slots
        gate_copy, up_copy = copies(i)
        gate_copy.wait()
        gate = jnp.dot(x, gate_buf[slot], preferred_element_type=jnp.float32)
        up_copy.wait()
        up = jnp.dot(x, up_buf[slot], preferred_element_type=jnp.float32)
        if i + slots < local:
            for copy in copies(i + slots):
                copy.start()
        if i == max(local - slots, 0):
            for j in range(down_slots):
                down_copy(j).start()
        expert = (first_ref[0] + i).astype(jnp.float32)
        weight = jnp.sum(jnp.where(named == expert, weights, 0.0), axis=1, keepdims=True)
        value = gate / (1.0 + jnp.exp(-gate)) * up * weight
        act_buf[:, i * hidden : (i + 1) * hidden] = jnp.where(
            weight == 0.0, 0.0, value
        ).astype(jnp.bfloat16)
    half = act_buf.shape[0] // 2
    for j in range(blocks):
        down_copy(j).wait()
        sums = jnp.dot(
            act_buf[...],
            down_buf[j % down_slots].reshape(local * hidden, width),
            preferred_element_type=jnp.float32,
        )
        if j + down_slots < blocks:
            down_copy(j + down_slots).start()
        at = pl.ds(j * width, width)
        keep_ref[:, at] = sums[:half]
        send_ref[:, at] = sums[half:].astype(jnp.bfloat16)


def experts(x, scale, gate, up, down, first, chosen):
    count = x.shape[0]
    local, feat, hidden = gate.shape
    whole = pl.BlockSpec(memory_space=pltpu.VMEM)
    apart = pl.BlockSpec(memory_space=pl.ANY)
    slots = min(3, local)
    width = chunk_of(feat, 512)
    down_slots = (feat // width + 1) // 2
    buffer = pltpu.VMEM((slots, feat, hidden), gate.dtype)
    return pl.pallas_call(
        functools.partial(experts_kernel, chosen),
        in_specs=[pl.BlockSpec(memory_space=pltpu.SMEM), whole, whole, apart, apart, apart],
        out_shape=[
            jax.ShapeDtypeStruct((count, LANES), jnp.float32),
            jax.ShapeDtypeStruct((count // 2, feat), jnp.float32),
            jax.ShapeDtypeStruct((count // 2, feat), jnp.bfloat16),
        ],
        scratch_shapes=[
            pltpu.VMEM((count, local * hidden), jnp.bfloat16),
            buffer,
            buffer,
            pltpu.VMEM((down_slots, local, hidden, width), down.dtype),
            pltpu.SemaphoreType.DMA((2, slots)),
            pltpu.SemaphoreType.DMA((down_slots,)),
        ],
        compiler_params=pltpu.CompilerParams(vmem_limit_bytes=VMEM_LIMIT),
        cost_estimate=pl.CostEstimate(
            flops=6 * count * local * feat * hidden,
            bytes_accessed=6 * local * feat * hidden,
            transcendentals=count * local * hidden,
        ),
        name="experts",
    )(first, x, scale.reshape(1, feat), gate, up, down)


def shared_out_kernel(sizes, branch_ref, down_ref, *refs):
    outer, spread, rows = sizes
    act_refs, (keep_ref, send_ref) = refs[:spread], refs[spread:]
    act = jnp.concatenate([ref[...] for ref in act_refs], axis=0)
    sums = jnp.dot(act, down_ref[...], preferred_element_type=jnp.float32)
    width = sums.shape[1]
    sums = jnp.swapaxes(sums.reshape(spread, outer, rows, width), 0, 1)
    sums = sums.reshape(outer * spread * rows, width) * branch_ref[:, :1]
    half = sums.shape[0] // 2
    keep_ref[...] = sums[:half]
    send_ref[...] = sums[half:].astype(jnp.bfloat16)


def shared_out(branch, down, acts, rows):
    count, spread = branch.shape[0], len(acts)
    outer = count // (spread * rows)
    shape = (count // 2, down.shape[1])
    return pl.pallas_call(
        functools.partial(shared_out_kernel, (outer, spread, rows)),
        out_shape=[
            jax.ShapeDtypeStruct(shape, jnp.float32),
            jax.ShapeDtypeStruct(shape, jnp.bfloat16),
        ],
        compiler_params=pltpu.CompilerParams(vmem_limit_bytes=VMEM_LIMIT),
        cost_estimate=pl.CostEstimate(
            flops=2 * count * down.shape[0] * down.shape[1],
            bytes_accessed=2 * down.shape[0] * down.shape[1],
            transcendentals=0,
        ),
        name="shared_out",
    )(branch, down, *acts)


def narrow_sum(keep, send):
    return chip_sum(keep + core_swap(send).astype(jnp.float32))


def chip_sum(total):
    chips = lax.axis_size("narrow") // 2
    part = total.shape[0] // chips
    result = total[:part]
    for d in range(1, chips):
        piece = total[d * part : (d + 1) * part].astype(jnp.bfloat16)
        result = result + x_shift(piece, -d).astype(jnp.float32)
    return result


def body(
    tokens,
    expert_ids,
    route_weights,
    expert_gate,
    expert_up,
    expert_down,
    shared_gate,
    shared_up,
    shared_down,
    shared_scale,
):
    rows, feat = tokens.shape
    spread = lax.axis_size("expert")
    here = lax.axis_index("expert")
    local = expert_gate.shape[0]
    depth = shared_gate.shape[0]
    chosen = expert_ids.shape[1]
    own = jnp.concatenate(
        [
            tokens,
            expert_ids.astype(jnp.bfloat16),
            route_weights,
            jnp.zeros((rows, LANES - 2 * chosen), jnp.bfloat16),
        ],
        axis=1,
    )
    column = jnp.concatenate(gather_column([own] * spread), axis=0)
    part = lax.dynamic_slice_in_dim(column, here * depth, depth, axis=1)
    early = jnp.concatenate([part, column[:, feat:]], axis=1)
    early, up = join(gather_plane(early), load([shared_up], shared_up.shape[0]))
    parts = [piece[:, :depth] for piece in early]
    parts = parts + [core_swap(piece) for piece in parts]
    hidden_own, *hidden_parts = shared_in(parts, shared_gate, *up, rows)
    plane, (hidden_own,) = join(gather_plane(column[:, :feat]), [hidden_own])
    plane = [
        jnp.concatenate([piece, rest[:, depth:]], axis=1) for piece, rest in zip(plane, early)
    ]
    x = both_cores(jnp.concatenate(plane, axis=0))

    first = (here * local).astype(jnp.int32).reshape(1)
    branch, keep, send = experts(
        x, shared_scale, expert_gate, expert_up, expert_down, first, chosen
    )
    arrived = [z_shift(piece, -d) for d, piece in enumerate(hidden_parts, 1)]
    arrived, (keep, send) = join(arrived, [keep, send])
    hidden = hidden_own.astype(jnp.float32)
    for piece in arrived:
        hidden = hidden + piece.astype(jnp.float32)
    shared_act = (jax.nn.silu(hidden[0]) * hidden[1]).astype(jnp.bfloat16)
    acts = gather_column([shared_act] * spread)
    routed = keep + core_swap(send).astype(jnp.float32)
    middle = feat // LANES // 2 * LANES
    routed = [chip_sum(routed[:, :middle]), chip_sum(routed[:, middle:])]
    down = join([shared_down, shared_act])[0][:1]
    acts, down = join(acts, load(down, shared_down.shape[0]))
    part = shared_out(branch, *down, acts, rows)
    part, routed = join(part, routed)
    total, part = jnp.concatenate(routed, axis=1), narrow_sum(*part)
    at = here * part.shape[1]
    part = part + lax.dynamic_slice_in_dim(total, at, part.shape[1], axis=1)
    total = lax.dynamic_update_slice_in_dim(total, part, at, axis=1)
    out = total[:rows]
    for d in range(1, spread):
        piece = total[d * rows : (d + 1) * rows].astype(jnp.bfloat16)
        out = out + z_shift(piece, -d).astype(jnp.float32)
    return out.astype(jnp.bfloat16)


def solution(mesh):
    return jax.shard_map(
        body,
        mesh=mesh,
        in_specs=(
            P(("groups", "expert", "narrow"), None),
            P(("groups", "expert", "narrow"), None),
            P(("groups", "expert", "narrow"), None),
            P("expert", None, "narrow"),
            P("expert", None, "narrow"),
            P("expert", "narrow", None),
            P("expert", "narrow"),
            P("expert", "narrow"),
            P("narrow", "expert"),
            P(),
        ),
        out_specs=P(("groups", "expert", "narrow"), None),
        check_vma=False,
    )
```

```python
import functools
import math

import jax
import jax.numpy as jnp
from jax import lax
from jax.experimental import pallas as pl
from jax.experimental.pallas import tpu as pltpu
from jax.sharding import PartitionSpec as P

EXPERTS = 32
LANES = 128
VMEM_LIMIT = 48 * 2**20
VMEM_SMALL = 8 * 2**20


def chunk_of(width, most):
    best = width
    for size in range(LANES, most + 1, LANES):
        if width % size == 0:
            best = size
    return best


def z_shift(value, step):
    spread = lax.axis_size("expert")
    return lax.ppermute(value, "expert", [(i, (i + step) % spread) for i in range(spread)])


def x_shift(value, step):
    size = lax.axis_size("narrow")
    return lax.ppermute(value, "narrow", [(i, (i + 2 * step) % size) for i in range(size)])


def core_swap(value):
    size = lax.axis_size("narrow")
    return lax.ppermute(value, "narrow", [(i, i ^ 1) for i in range(size)])


def gather_column(pieces):
    return [pieces[0]] + [z_shift(piece, d) for d, piece in enumerate(pieces) if d > 0]


def gather_plane(column):
    chips = lax.axis_size("narrow") // 2
    return [column] + [x_shift(column, d) for d in range(1, chips)]


def both_cores(plane):
    return jnp.concatenate([plane, core_swap(plane)], axis=0)


def join(*lists):
    values = iter(lax.optimization_barrier([value for part in lists for value in part]))
    return [[next(values) for _ in part] for part in lists]


def load_kernel(*refs):
    count = len(refs) // 2
    sources, targets, sems = refs[:count], refs[count:-1], refs[-1]
    copies = [
        pltpu.make_async_copy(source.at[pl.ds(0, target.shape[0])], target, sems.at[i])
        for i, (source, target) in enumerate(zip(sources, targets))
    ]
    for copy in copies:
        copy.start()
    for copy in copies:
        copy.wait()


def load(arrays, taken):
    shapes = [(taken, *value.shape[1:]) for value in arrays]
    return pl.pallas_call(
        load_kernel,
        in_specs=[pl.BlockSpec(memory_space=pl.ANY)] * len(arrays),
        out_shape=[
            jax.ShapeDtypeStruct(shape, value.dtype) for shape, value in zip(shapes, arrays)
        ],
        scratch_shapes=[pltpu.SemaphoreType.DMA((len(arrays),))],
        compiler_params=pltpu.CompilerParams(vmem_limit_bytes=VMEM_SMALL),
        cost_estimate=pl.CostEstimate(
            flops=0,
            bytes_accessed=sum(2 * math.prod(shape) for shape in shapes),
            transcendentals=0,
        ),
        name="load",
    )(*arrays)


def shared_in_kernel(sizes, width, gate_ref, up_ref, *refs):
    outer, spread, rows = sizes
    x_refs, out_refs = refs[:outer], refs[outer : outer + spread]
    x_buf, sems = refs[outer + spread :]
    copies = [
        pltpu.make_async_copy(ref, x_buf.at[i], sems.at[i]) for i, ref in enumerate(x_refs)
    ]
    for copy in copies:
        copy.start()
    for copy in copies:
        copy.wait()
    x = x_buf[...].reshape(outer * spread * rows, x_buf.shape[2])
    for half, ref in enumerate((gate_ref, up_ref)):
        for j in range(ref.shape[1] // width):
            columns = pl.ds(j * width, width)
            sums = jnp.dot(x, ref[:, columns], preferred_element_type=jnp.float32)
            sums = sums.reshape(outer, spread, rows, width)
            for d in range(spread):
                block = sums[:, d].reshape(outer * rows, width)
                out_refs[d][half, :, columns] = block.astype(jnp.bfloat16)


def shared_in(pieces, gate, up, rows):
    depth, hidden = gate.shape
    outer, spread = len(pieces), lax.axis_size("expert")
    count = outer * spread * rows
    whole = pl.BlockSpec(memory_space=pltpu.VMEM)
    apart = pl.BlockSpec(memory_space=pl.ANY)
    return pl.pallas_call(
        functools.partial(shared_in_kernel, (outer, spread, rows), chunk_of(hidden, 512)),
        in_specs=[whole, whole] + [apart] * outer,
        out_shape=[jax.ShapeDtypeStruct((2, outer * rows, hidden), jnp.bfloat16)] * spread,
        scratch_shapes=[
            pltpu.VMEM((outer, spread * rows, depth), gate.dtype),
            pltpu.SemaphoreType.DMA((outer,)),
        ],
        compiler_params=pltpu.CompilerParams(vmem_limit_bytes=VMEM_SMALL),
        cost_estimate=pl.CostEstimate(
            flops=4 * count * depth * hidden,
            bytes_accessed=4 * count * hidden,
            transcendentals=0,
        ),
        name="shared_in",
    )(gate, up, *pieces)


def experts_kernel(chosen, first_ref, x_ref, scale_ref, gate_ref, up_ref, down_ref, *refs):
    branch_ref, keep_ref, send_ref = refs[:3]
    act_buf, gate_buf, up_buf, down_buf, sems, down_sems = refs[3:]
    local, feat, hidden = gate_ref.shape
    slots, (down_slots, _, _, width) = gate_buf.shape[0], down_buf.shape
    blocks = feat // width

    def copies(i):
        slot = i % slots
        return [
            pltpu.make_async_copy(ref.at[i], buf.at[slot], sems.at[half, slot])
            for half, (ref, buf) in enumerate(((gate_ref, gate_buf), (up_ref, up_buf)))
        ]

    def down_copy(j):
        slot = j % down_slots
        return pltpu.make_async_copy(
            down_ref.at[:, :, pl.ds(j * width, width)], down_buf.at[slot], down_sems.at[slot]
        )

    for i in range(slots):
        for copy in copies(i):
            copy.start()
    inner = jnp.sum(x_ref[:, :feat].astype(jnp.float32) * scale_ref[...], axis=1, keepdims=True)
    branch_ref[...] = jnp.broadcast_to(1.0 / (1.0 + jnp.exp(-inner)), branch_ref.shape)
    route = x_ref[:, feat:].astype(jnp.float32)
    named, weights = route[:, :chosen], route[:, chosen : 2 * chosen]
    x = x_ref[:, :feat]
    for i in range(local):
        slot = i % slots
        gate_copy, up_copy = copies(i)
        gate_copy.wait()
        gate = jnp.dot(x, gate_buf[slot], preferred_element_type=jnp.float32)
        up_copy.wait()
        up = jnp.dot(x, up_buf[slot], preferred_element_type=jnp.float32)
        if i + slots < local:
            for copy in copies(i + slots):
                copy.start()
        if i == max(local - slots, 0):
            for j in range(down_slots):
                down_copy(j).start()
        expert = (first_ref[0] + i).astype(jnp.float32)
        weight = jnp.sum(jnp.where(named == expert, weights, 0.0), axis=1, keepdims=True)
        value = gate / (1.0 + jnp.exp(-gate)) * up * weight
        act_buf[:, i * hidden : (i + 1) * hidden] = jnp.where(
            weight == 0.0, 0.0, value
        ).astype(jnp.bfloat16)
    half = act_buf.shape[0] // 2
    for j in range(blocks):
        down_copy(j).wait()
        sums = jnp.dot(
            act_buf[...],
            down_buf[j % down_slots].reshape(local * hidden, width),
            preferred_element_type=jnp.float32,
        )
        if j + down_slots < blocks:
            down_copy(j + down_slots).start()
        at = pl.ds(j * width, width)
        keep_ref[:, at] = sums[:half]
        send_ref[:, at] = sums[half:].astype(jnp.bfloat16)


def experts(x, scale, gate, up, down, first, chosen):
    count = x.shape[0]
    local, feat, hidden = gate.shape
    whole = pl.BlockSpec(memory_space=pltpu.VMEM)
    apart = pl.BlockSpec(memory_space=pl.ANY)
    slots = min(3, local)
    width = chunk_of(feat, 512)
    down_slots = (feat // width + 1) // 2
    buffer = pltpu.VMEM((slots, feat, hidden), gate.dtype)
    return pl.pallas_call(
        functools.partial(experts_kernel, chosen),
        in_specs=[pl.BlockSpec(memory_space=pltpu.SMEM), whole, whole, apart, apart, apart],
        out_shape=[
            jax.ShapeDtypeStruct((count, LANES), jnp.float32),
            jax.ShapeDtypeStruct((count // 2, feat), jnp.float32),
            jax.ShapeDtypeStruct((count // 2, feat), jnp.bfloat16),
        ],
        scratch_shapes=[
            pltpu.VMEM((count, local * hidden), jnp.bfloat16),
            buffer,
            buffer,
            pltpu.VMEM((down_slots, local, hidden, width), down.dtype),
            pltpu.SemaphoreType.DMA((2, slots)),
            pltpu.SemaphoreType.DMA((down_slots,)),
        ],
        compiler_params=pltpu.CompilerParams(vmem_limit_bytes=VMEM_LIMIT),
        cost_estimate=pl.CostEstimate(
            flops=6 * count * local * feat * hidden,
            bytes_accessed=6 * local * feat * hidden,
            transcendentals=count * local * hidden,
        ),
        name="experts",
    )(first, x, scale.reshape(1, feat), gate, up, down)


def shared_out_kernel(sizes, branch_ref, down_ref, *refs):
    outer, spread, rows = sizes
    act_refs, (keep_ref, send_ref) = refs[:spread], refs[spread:]
    act = jnp.concatenate([ref[...] for ref in act_refs], axis=0)
    sums = jnp.dot(act, down_ref[...], preferred_element_type=jnp.float32)
    width = sums.shape[1]
    sums = jnp.swapaxes(sums.reshape(spread, outer, rows, width), 0, 1)
    sums = sums.reshape(outer * spread * rows, width) * branch_ref[:, :1]
    half = sums.shape[0] // 2
    keep_ref[...] = sums[:half]
    send_ref[...] = sums[half:].astype(jnp.bfloat16)


def shared_out(branch, down, acts, rows):
    count, spread = branch.shape[0], len(acts)
    outer = count // (spread * rows)
    shape = (count // 2, down.shape[1])
    return pl.pallas_call(
        functools.partial(shared_out_kernel, (outer, spread, rows)),
        out_shape=[
            jax.ShapeDtypeStruct(shape, jnp.float32),
            jax.ShapeDtypeStruct(shape, jnp.bfloat16),
        ],
        compiler_params=pltpu.CompilerParams(vmem_limit_bytes=VMEM_LIMIT),
        cost_estimate=pl.CostEstimate(
            flops=2 * count * down.shape[0] * down.shape[1],
            bytes_accessed=2 * down.shape[0] * down.shape[1],
            transcendentals=0,
        ),
        name="shared_out",
    )(branch, down, *acts)


def peers_sum(keep, send):
    size = lax.axis_size("narrow")
    chips = size // 2
    part = keep.shape[0] // chips
    result = keep[:part]
    for d in range(chips):
        rows = slice(d * part, (d + 1) * part)
        if d > 0:
            piece = keep[rows].astype(jnp.bfloat16)
            result = result + x_shift(piece, -d).astype(jnp.float32)
        pairs = [(i, ((i - 2 * d) % size) ^ 1) for i in range(size)]
        result = result + lax.ppermute(send[rows], "narrow", pairs).astype(jnp.float32)
    return result


def chip_sum(total):
    chips = lax.axis_size("narrow") // 2
    part = total.shape[0] // chips
    result = total[:part]
    for d in range(1, chips):
        piece = total[d * part : (d + 1) * part].astype(jnp.bfloat16)
        result = result + x_shift(piece, -d).astype(jnp.float32)
    return result


def body(
    tokens,
    expert_ids,
    route_weights,
    expert_gate,
    expert_up,
    expert_down,
    shared_gate,
    shared_up,
    shared_down,
    shared_scale,
):
    rows, feat = tokens.shape
    spread = lax.axis_size("expert")
    here = lax.axis_index("expert")
    local = expert_gate.shape[0]
    depth = shared_gate.shape[0]
    chosen = expert_ids.shape[1]
    own = jnp.concatenate(
        [
            tokens,
            expert_ids.astype(jnp.bfloat16),
            route_weights,
            jnp.zeros((rows, LANES - 2 * chosen), jnp.bfloat16),
        ],
        axis=1,
    )
    column = jnp.concatenate(gather_column([own] * spread), axis=0)
    part = lax.dynamic_slice_in_dim(column, here * depth, depth, axis=1)
    early = jnp.concatenate([part, column[:, feat:]], axis=1)
    early, up = join(gather_plane(early), load([shared_up], shared_up.shape[0]))
    parts = [piece[:, :depth] for piece in early]
    parts = parts + [core_swap(piece) for piece in parts]
    hidden_own, *hidden_parts = shared_in(parts, shared_gate, *up, rows)
    plane, (hidden_own,) = join(gather_plane(column[:, :feat]), [hidden_own])
    plane = [
        jnp.concatenate([piece, rest[:, depth:]], axis=1) for piece, rest in zip(plane, early)
    ]
    x = both_cores(jnp.concatenate(plane, axis=0))

    first = (here * local).astype(jnp.int32).reshape(1)
    branch, keep, send = experts(
        x, shared_scale, expert_gate, expert_up, expert_down, first, chosen
    )
    arrived = [z_shift(piece, -d) for d, piece in enumerate(hidden_parts, 1)]
    arrived, (keep, send) = join(arrived, [keep, send])
    hidden = hidden_own.astype(jnp.float32)
    for piece in arrived:
        hidden = hidden + piece.astype(jnp.float32)
    shared_act = (jax.nn.silu(hidden[0]) * hidden[1]).astype(jnp.bfloat16)
    acts = gather_column([shared_act] * spread)
    routed = keep + core_swap(send).astype(jnp.float32)
    middle = feat // LANES // 2 * LANES
    routed = [chip_sum(routed[:, :middle]), chip_sum(routed[:, middle:])]
    down = join([shared_down, shared_act])[0][:1]
    acts, down = join(acts, load(down, shared_down.shape[0]))
    part = shared_out(branch, *down, acts, rows)
    part, routed = join(part, routed)
    total, part = jnp.concatenate(routed, axis=1), peers_sum(*part)
    at = here * part.shape[1]
    part = part + lax.dynamic_slice_in_dim(total, at, part.shape[1], axis=1)
    total = lax.dynamic_update_slice_in_dim(total, part, at, axis=1)
    out = total[:rows]
    for d in range(1, spread):
        piece = total[d * rows : (d + 1) * rows].astype(jnp.bfloat16)
        out = out + z_shift(piece, -d).astype(jnp.float32)
    return out.astype(jnp.bfloat16)


def solution(mesh):
    return jax.shard_map(
        body,
        mesh=mesh,
        in_specs=(
            P(("groups", "expert", "narrow"), None),
            P(("groups", "expert", "narrow"), None),
            P(("groups", "expert", "narrow"), None),
            P("expert", None, "narrow"),
            P("expert", None, "narrow"),
            P("expert", "narrow", None),
            P("expert", "narrow"),
            P("expert", "narrow"),
            P("narrow", "expert"),
            P(),
        ),
        out_specs=P(("groups", "expert", "narrow"), None),
        check_vma=False,
    )
```
